32 devices in a mesh: parts: 2 (over y), dp: 4 (over z), tensor: 4 (over x, core).
Axes of the slice: x: 2, y: 2, z: 4, core: 2. Of those that a mesh axis runs over, the one named last changes fastest.
Arguments:
- tokens: bfloat16 [40, 256, 5120], P(('parts', 'dp'), 'tensor'), parts along dimension 0, may hold values from -25 to 25
- norm_gain: float32 [5120], replicated, may hold values from 0.1 to 1.9
- norm_bias: float32 [5120], replicated, may hold values from -3 to 3
- qkv_weight: bfloat16 [5120, 8, 3, 128], P(None, 'tensor'), may hold values from -8 to 8
- qkv_bias: float32 [8, 3, 128], P('tensor'), may hold values from -3 to 3
- out_weight: bfloat16 [8, 128, 5120], P('tensor'), may hold values from -0.5 to 0.5
- out_bias: float32 [5120], replicated, may hold values from -3 to 3
- lengths: int32 [24, 3], P('parts'), parts along dimension 0, may hold values from 50 to 156, as said below
- source_bin: int32 [24], P('parts'), parts along dimension 0, may hold values from 0 to 19, as said below
Outputs:
- refreshed: bfloat16 [24, 256, 5120], P(('parts', 'dp'), 'tensor'), parts along dimension 0
The draws below stay inside these ranges and needn't reach their ends.
There are 2 independent parts, one for each index of `parts`. The reference program is written for one: setup_inputs(seed, part) draws one part's arguments, and reference() takes and returns one part's arrays. A program takes and returns all parts, laid end to end along the dimension named above; an argument that names none is the same for every part. Nothing has to cross between parts.
Inputs may be any that keep to these rules, and one draw needn't show every extreme that they name: Bucket b belongs to data group b // 3. The 3 lengths of a bucket add up to 256 or less, and to exactly 256 in one bucket of every data group. In every draw some protein has 156 residues and some 50. source_bin[b] is data group times 5 plus a bin number; no bin holds two buckets. Half of the data groups hold 5 buckets, their own 3 and 2 of one partner group; each partner keeps one of its own buckets; the other bins are empty and their slots are not read. So every data group sends at most 2 buckets, all to one group.
All inputs are finite; a program needn't handle non-finite values.
Results may differ from the reference program's by a relative error of at most 0.01.
Values may be sent and summed in bfloat16 or wider, within the bound.
No kernel may reach another device: no remote copies, remote signals or barrier semaphores. Data moves between devices by JAX's collectives and lax.ppermute only.
A program may use at most 128 MiB of HBM per device.

```python
import jax
import jax.numpy as jnp
from jax import lax

D = 5120
HD = 128
HEADS = 8
BLEN = 256
K = 3
MINLEN = 50
NBK = 3
NSB = 5
SRC_BINS = 20
N_DP = 4
N_TENSOR = 4


def draw_tokens(key, part):
    key = jax.random.fold_in(key, 5)
    keys = jax.random.split(key, 1)
    result = jnp.clip(jax.random.normal(keys[0], (SRC_BINS, BLEN, D), jnp.float32), -6.0, 6.0)
    return result.astype(jnp.bfloat16)


def draw_qkv_weight(key, part):
    key = jax.random.fold_in(key, 9)
    keys = jax.random.split(key, 3)
    scale = D ** (-0.5)
    query_part = jnp.clip(jax.random.normal(keys[0], (D, HEADS, HD), jnp.float32), -6.0, 6.0) * scale
    key_part = jnp.clip(jax.random.normal(keys[1], (D, HEADS, HD), jnp.float32), -6.0, 6.0) * scale
    value_part = jnp.clip(jax.random.normal(keys[2], (D, HEADS, HD), jnp.float32), -6.0, 6.0) * scale
    return jnp.stack([query_part, key_part, value_part], axis=2).astype(jnp.bfloat16)


def draw_lengths(key, part):
    key = jax.random.fold_in(key, 11)
    key_total, key_full, key_cut = jax.random.split(key, 3)
    floor_sum = K * MINLEN
    bucket_total = N_DP * NBK
    totals = jax.random.randint(key_total, (N_DP, NBK), floor_sum, BLEN + 1, jnp.int32)
    full_bucket = jax.random.randint(key_full, (N_DP, 1), 0, NBK, jnp.int32)
    column = jnp.arange(NBK, dtype=jnp.int32)[None, :]
    totals = jnp.where(column == full_bucket, BLEN, totals).reshape(bucket_total)
    surplus = (totals - floor_sum).astype(jnp.int32)
    cuts = jax.random.randint(key_cut, (bucket_total, K - 1), 0, 1 + surplus[:, None], jnp.int32)
    cuts = jnp.sort(cuts, axis=1)
    edges = jnp.concatenate([jnp.zeros((bucket_total, 1), jnp.int32), cuts, surplus[:, None]], axis=1)
    extras = edges[:, 1:] - edges[:, :-1]
    extreme = jnp.zeros((K,), jnp.int32).at[0].set(BLEN - floor_sum)
    bucket_ids = jnp.arange(bucket_total, dtype=jnp.int32)
    extras = jnp.where((bucket_ids == full_bucket[0, 0])[:, None], extreme[None, :], extras)
    return (MINLEN + extras).astype(jnp.int32)


def draw_source_bin(key, part):
    key = jax.random.fold_in(key, 13)
    key_order, key_keep, key_bins = jax.random.split(key, 3)
    half_count = N_DP // 2
    ordering = jax.random.permutation(key_order, N_DP).astype(jnp.int32)
    rank_of = jnp.argsort(ordering).astype(jnp.int32)
    is_light = rank_of >= half_count
    partner = ordering[jnp.where(is_light, rank_of - half_count, 0)]
    kept_bucket = jax.random.randint(key_keep, (N_DP,), 0, NBK, jnp.int32)
    group_ids = jnp.broadcast_to(jnp.arange(N_DP, dtype=jnp.int32)[:, None], (N_DP, NBK))
    bucket = jnp.broadcast_to(jnp.arange(NBK, dtype=jnp.int32)[None, :], (N_DP, NBK))
    leaving = is_light[group_ids] & (bucket != kept_bucket[group_ids])
    holder = jnp.where(leaving, partner[group_ids], group_ids)
    later = (bucket > kept_bucket[group_ids]).astype(jnp.int32)
    hold_rank = jnp.where(leaving, NBK + bucket - later, jnp.where(is_light[group_ids], 0, bucket))
    shuffles = jax.vmap(lambda sub_key: jax.random.permutation(sub_key, NSB))(jax.random.split(key_bins, N_DP)).astype(jnp.int32)
    bin_slot = shuffles[holder, hold_rank]
    return (holder * NSB + bin_slot).reshape(N_DP * NBK).astype(jnp.int32)


def level_of(rng, extent, pieces, smallest, high):
    def one(dim, blocks):
        heights = jax.random.uniform(jax.random.fold_in(jax.random.fold_in(rng, 6), dim), (blocks,), jnp.float32, smallest / len(pieces), high / len(pieces))
        return jnp.repeat(jnp.exp(heights), extent[dim] // blocks).reshape((-1,) + (1,) * (len(extent) - dim - 1))

    level = one(*pieces[0])
    for cut in pieces[1:]:
        level = level * one(*cut)
    return level


def normal_values(own_key, extent, deviation, reach, pieces=(), held_as=jnp.bfloat16):
    array = deviation * jax.random.normal(own_key, extent, jnp.float32)
    if pieces:
        array = array * level_of(own_key, extent, pieces, -0.22, 0.18)
    return jnp.clip(array, -reach, reach).astype(held_as)


def setup_inputs(seed: int = 0, part: int = 0) -> dict:
    seeds = jax.random.split(jax.random.key(seed), 10)
    part_keys = jax.random.split(jax.random.fold_in(seeds[9], part), 10)
    return {
        "tokens": draw_tokens(jax.random.fold_in(jax.random.fold_in(seeds[9], part), 71), part),
        "norm_gain": jnp.clip(1.0 + 0.18 * jax.random.normal(seeds[1], (D,), jnp.float32), 0.1, 1.9),
        "norm_bias": normal_values(seeds[2], (D,), 0.5, 3.0, (), jnp.float32),
        "qkv_weight": draw_qkv_weight(jax.random.fold_in(seeds[9], 71), part),
        "qkv_bias": normal_values(seeds[4], (HEADS, 3, HD), 0.5, 3.0, ((0, 4),), jnp.float32),
        "out_weight": normal_values(seeds[5], (HEADS, HD, D), HD ** -0.5, 0.5, ((0, 4),)),
        "out_bias": normal_values(seeds[6], (D,), 0.5, 3.0, (), jnp.float32),
        "lengths": draw_lengths(jax.random.fold_in(jax.random.fold_in(seeds[9], part), 71), part),
        "source_bin": draw_source_bin(jax.random.fold_in(jax.random.fold_in(seeds[9], part), 71), part),
    }


def protein_layout(bucket_lengths, full_rows):
    end_points = jnp.cumsum(bucket_lengths, axis=-1).astype(jnp.int32)
    starts = (end_points - bucket_lengths).astype(jnp.int32)
    row_index = jnp.arange(full_rows, dtype=jnp.int32)
    member = lax.optimization_barrier(jnp.sum((row_index[:, None] >= end_points[..., None, :]).astype(jnp.int32), axis=-1)).astype(jnp.int32)
    slots = jnp.arange(bucket_lengths.shape[-1], dtype=jnp.int32)
    picked = member[..., None] == slots
    offset = lax.optimization_barrier(jnp.sum(jnp.where(picked, starts[..., None, :], 0), axis=-1)).astype(jnp.int32)
    position = (row_index - offset).astype(jnp.int32)
    return (member, position)

def rotate(vectors, position):
    half_size = vectors.shape[-1] // 2
    frequency = 10000.0 ** (-2.0 * jnp.arange(half_size, dtype=jnp.float32) / vectors.shape[-1])
    angles = position.astype(jnp.float32)[..., None] * frequency
    angles = jnp.concatenate([angles, angles], axis=-1)[..., None, :]
    leading = vectors[..., :half_size]
    trailing = vectors[..., half_size:]
    turned = jnp.concatenate([-trailing, leading], axis=-1)
    return vectors * jnp.cos(angles) + turned * jnp.sin(angles)

def refresh(blocks, bucket_lengths, norm_gain, norm_bias, qkv_weight, qkv_bias, out_weight, out_bias):
    full_rows = blocks.shape[0]
    protein_slots = bucket_lengths.shape[-1]
    member, position = protein_layout(bucket_lengths, full_rows)
    widened = blocks.astype(jnp.float32)
    average = lax.optimization_barrier(jnp.mean(widened, axis=-1, keepdims=True))
    spread = lax.optimization_barrier(jnp.mean((widened - average) ** 2, axis=-1, keepdims=True))
    normed = ((widened - average) * lax.rsqrt(spread + 1e-05) * norm_gain + norm_bias).astype(jnp.bfloat16)
    head_count = qkv_weight.shape[1]
    head_size = qkv_weight.shape[3]
    width = qkv_weight.shape[0]
    flat_qkv = qkv_weight.reshape(width, head_count * 3 * head_size)
    projected = jnp.dot(normed, flat_qkv, preferred_element_type=jnp.float32).reshape(full_rows, head_count, 3, head_size) + qkv_bias
    queries = rotate(projected[:, :, 0] * head_size ** (-0.5), position).astype(jnp.bfloat16)
    key_rows = rotate(projected[:, :, 1], position).astype(jnp.bfloat16)
    values = projected[:, :, 2].astype(jnp.bfloat16)
    scores = jnp.einsum('qhd,khd->hqk', queries.astype(jnp.float32), key_rows.astype(jnp.float32))
    allowed = (member[:, None] == member[None, :]) & (member[None, :] < protein_slots)
    masked = jnp.where(allowed[None], scores, jnp.float32(-1e+30))
    highest = lax.optimization_barrier(jnp.max(masked, axis=-1, keepdims=True))
    raised = jnp.exp(masked - highest)
    weights = (raised / lax.optimization_barrier(jnp.sum(raised, axis=-1, keepdims=True))).astype(jnp.bfloat16)
    context = jnp.einsum('hqk,khd->qhd', weights.astype(jnp.float32), values.astype(jnp.float32)).astype(jnp.bfloat16)
    group_width = head_count // N_TENSOR * head_size
    context_groups = jnp.transpose(context.reshape(full_rows, N_TENSOR, group_width), (1, 0, 2))
    weight_groups = out_weight.reshape(N_TENSOR, group_width, width)

    def add_group(running, operand):
        term = jnp.dot(operand[0], operand[1], preferred_element_type=jnp.float32)
        rounded = lax.optimization_barrier(term.astype(jnp.bfloat16))
        return (running + rounded.astype(jnp.float32), None)
    head_sum, unused = lax.scan(add_group, jnp.zeros((full_rows, width), jnp.float32), (context_groups, weight_groups))
    result = jnp.where((member < protein_slots)[:, None], widened + head_sum + out_bias, jnp.float32(0.0))
    return result.astype(jnp.bfloat16)

def reference(tokens, norm_gain, norm_bias, qkv_weight, qkv_bias, out_weight, out_bias, lengths, source_bin):
    gathered = jnp.take(tokens, source_bin.astype(jnp.int32), axis=0)

    def one_bucket(operand):
        return refresh(operand[0], operand[1], norm_gain, norm_bias, qkv_weight, qkv_bias, out_weight, out_bias)
    return lax.map(one_bucket, (gathered, lengths))
```

```python
import jax
import jax.numpy as jnp
from jax import lax
from jax.sharding import PartitionSpec as P


def exchange(value, axis, mask):
    size = lax.axis_size(axis)
    return lax.ppermute(value, axis, [(i, i ^ mask) for i in range(size)])


def masks_of(size):
    mask = size // 2
    result = []
    while mask:
        result.append(mask)
        mask //= 2
    return result


def gather_xor(own):
    pieces = {0: own}
    for mask in masks_of(lax.axis_size("tensor")):
        for j in list(pieces):
            pieces[j | mask] = exchange(pieces[j], "tensor", mask)
    return pieces


def layout_rows(bucket_lengths, rows):
    ends = jnp.cumsum(bucket_lengths, axis=-1)
    starts = ends - bucket_lengths
    member = jnp.sum((rows[:, None] >= ends[:, None, :]).astype(jnp.int32), axis=-1)
    picked = member[..., None] == jnp.arange(bucket_lengths.shape[-1], dtype=jnp.int32)
    position = rows - jnp.sum(jnp.where(picked, starts[:, None, :], 0), axis=-1)
    return member, position


def rotate(vectors, cosine, sine):
    half = vectors.shape[-1] // 2
    turned = jnp.concatenate([-vectors[..., half:], vectors[..., :half]], axis=-1)
    return vectors * cosine + turned * sine


def normalise(block, gain, bias):
    widened = block.astype(jnp.float32)
    average = jnp.mean(widened, axis=-1, keepdims=True)
    spread = jnp.mean((widened - average) ** 2, axis=-1, keepdims=True)
    return ((widened - average) * lax.rsqrt(spread + 1e-05) * gain + bias).astype(jnp.bfloat16)


def attend(pieces, weight, bias, member, position, slots):
    parts, heads, size = bias.shape
    rows = jnp.concatenate([pieces[j] for j in range(len(pieces))], axis=0)
    projected = jnp.dot(rows, weight, preferred_element_type=jnp.float32)
    projected = projected.reshape(-1, parts, heads, size) + bias
    frequency = 10000.0 ** (-2.0 * jnp.arange(size // 2, dtype=jnp.float32) / size)
    angles = position.astype(jnp.float32)[:, None] * frequency
    angles = jnp.concatenate([angles, angles], axis=-1)[:, None, :]
    cosine, sine = jnp.cos(angles), jnp.sin(angles)
    queries = rotate(projected[:, 0] * size ** (-0.5), cosine, sine).astype(jnp.bfloat16)
    key_rows = rotate(projected[:, 1], cosine, sine).astype(jnp.bfloat16)
    values = projected[:, 2].astype(jnp.bfloat16)
    scores = jnp.einsum("qhd,khd->hqk", queries, key_rows, preferred_element_type=jnp.float32)
    allowed = (member[:, None] == member[None, :]) & (member[None, :] < slots)
    masked = jnp.where(allowed, scores, jnp.float32(-1e30))
    highest = jnp.max(masked, axis=-1, keepdims=True)
    raised = jnp.exp(masked - highest)
    weights = (raised / jnp.sum(raised, axis=-1, keepdims=True)).astype(jnp.bfloat16)
    context = jnp.einsum("hqk,khd->qhd", weights, values, preferred_element_type=jnp.float32)
    return context.astype(jnp.bfloat16).reshape(len(pieces), -1, heads * size)


def return_context(context, swap):
    half = context.shape[-1] // 2
    turned = jnp.where(swap, jnp.roll(context, half, axis=-1), context)
    result = [context[0]]
    for j in range(1, context.shape[0]):
        result.append(exchange(context[j] if j == 1 else turned[j], "tensor", j))
    return jnp.concatenate(result, axis=-1)


def on_device(
    tokens, norm_gain, norm_bias, qkv_weight, qkv_bias, out_weight, out_bias, lengths, source_bin
):
    groups = lax.axis_size("dp")
    group = lax.axis_index("dp")
    tensors = lax.axis_size("tensor")
    rank = lax.axis_index("tensor")
    part_count = lax.axis_size("parts")
    part = lax.axis_index("parts")
    bins, shard_rows, width = tokens.shape
    slots = lengths.shape[-1]
    count = lengths.shape[0] // groups
    moved = bins - count
    heads, parts, size = qkv_weight.shape[1:]

    holder = source_bin // bins
    owner = jnp.arange(lengths.shape[0], dtype=jnp.int32) // count
    leaves = holder != owner
    mine = owner == group
    receives = jnp.any(mine & leaves)
    sends = jnp.any((holder == group) & leaves)
    partner = jnp.where(
        receives,
        jnp.max(jnp.where(mine & leaves, holder, 0)),
        jnp.max(jnp.where((holder == group) & leaves, owner, 0)),
    )
    order = jnp.argsort(jnp.where(mine, leaves.astype(jnp.int32), 2), stable=True)[:count]
    order = order.astype(jnp.int32)
    sent = jnp.argsort(jnp.logical_not((holder == group) & leaves), stable=True)[:moved]
    own_bins = jnp.take(source_bin, order) - group * bins
    own_bins = jnp.clip(own_bins, 0, bins - 1)
    sent_bins = jnp.clip(jnp.take(source_bin, sent) - group * bins, 0, bins - 1)
    outgoing = [
        lax.dynamic_index_in_dim(tokens, sent_bins[m], 0, keepdims=False) for m in range(moved)
    ]
    own = [lax.dynamic_index_in_dim(tokens, own_bins[m], 0, keepdims=False) for m in range(count)]
    my_lengths = jnp.take(lengths, order, axis=0)

    rows = jnp.concatenate(
        [
            (rank ^ j) * shard_rows + jnp.arange(shard_rows, dtype=jnp.int32)
            for j in range(tensors)
        ]
    )
    member, position = layout_rows(my_lengths, rows)

    depth = heads * size
    split = part_count == 2 and tensors > 2
    flat_out = out_weight.reshape(depth, width)
    swap = (part == 1) if split else False
    if split:
        first = lax.dynamic_slice_in_dim(flat_out, part * (depth // 2), depth // 2, 0)
    else:
        first = flat_out
    firsts = {0: first}
    for mask in masks_of(tensors)[:-1]:
        for j in list(firsts):
            firsts[j | mask] = exchange(firsts[j], "tensor", mask)
    del firsts[0]

    flat_qkv = jnp.transpose(qkv_weight, (0, 2, 1, 3)).reshape(width, parts * heads * size)
    bias = jnp.transpose(qkv_bias, (1, 0, 2))

    def finish(block, m):
        normed = normalise(block, norm_gain, norm_bias)
        context = attend(gather_xor(normed), flat_qkv, bias, member[m], position[m], slots)
        return return_context(context, swap)

    early = count - 1 if tensors <= 4 else 0

    def branch(pairs):
        def run():
            blocks = list(own)
            for m in range(moved):
                place = count - moved + m
                incoming = lax.ppermute(outgoing[m], "dp", pairs)
                blocks[place] = jnp.where(receives, incoming, own[place])
            return blocks, [finish(blocks[m], m) for m in range(early)]

        return run

    branches = []
    for k in range(1, groups):
        top = 1 << (k.bit_length() - 1)
        up = [(i, i ^ k) for i in range(groups) if not i & top]
        branches.append(branch(up))
        branches.append(branch([(d, s) for s, d in up]))
    apart = group ^ partner
    top = jnp.int32(1)
    for k in range(1, groups):
        top = jnp.where(apart == k, 1 << (k.bit_length() - 1), top)
    source = jnp.where(receives, partner, group)
    chosen = 2 * jnp.maximum(apart - 1, 0) + ((source & top) != 0).astype(jnp.int32)
    blocks, contexts = lax.switch(chosen, branches)
    contexts = contexts + [finish(blocks[m], m) for m in range(early, count)]

    rows_of = {0: [flat_out]}
    if tensors > 1:
        rows_of[1] = [exchange(flat_out, "tensor", 1)]
    for j in firsts:
        held = [firsts[j]]
        if split:
            held.append(exchange(firsts[j], "parts", 1))
        rows_of[j] = held
        rows_of[j | 1] = [exchange(h, "tensor", 1) for h in held]
    contexts = jnp.stack(contexts)
    head_sum = jnp.float32(0.0)
    place = 0
    for held in (h for j in range(tensors) for h in rows_of[j]):
        taken = contexts[:, :, place : place + held.shape[0]]
        head_sum = head_sum + jnp.dot(taken, held, preferred_element_type=jnp.float32)
        place += held.shape[0]
    widened = jnp.stack(blocks).astype(jnp.float32)
    local_member = member[:, :shard_rows]
    result = jnp.where(
        (local_member < slots)[..., None], widened + head_sum + out_bias, jnp.float32(0.0)
    ).astype(jnp.bfloat16)
    return jnp.take(result, jnp.argsort(order), axis=0)


def solution(mesh):
    return jax.shard_map(
        on_device,
        mesh=mesh,
        in_specs=(
            P(("parts", "dp"), "tensor", None),
            P(),
            P(),
            P(None, "tensor", None, None),
            P("tensor", None, None),
            P("tensor", None, None),
            P(),
            P("parts", None),
            P("parts"),
        ),
        out_specs=P(("parts", "dp"), "tensor", None),
        check_vma=False,
    )
```

```python
import functools

import jax
import jax.numpy as jnp
from jax import lax
from jax.experimental import pallas as pl
from jax.experimental.pallas import tpu as pltpu
from jax.sharding import PartitionSpec as P

MIB = 1 << 20
CHOSEN, RECEIVES, GROUP, RANK, PART, FIRST = 0, 1, 2, 3, 4, 8
ANY = pl.BlockSpec(memory_space=pl.ANY)
SMEM = pl.BlockSpec(memory_space=pltpu.SMEM)
VMEM = pl.BlockSpec(memory_space=pltpu.VMEM)


def exchange(value, axis, mask):
    size = lax.axis_size(axis)
    return lax.ppermute(value, axis, [(i, i ^ mask) for i in range(size)])


def masks_of(size):
    mask = size // 2
    result = []
    while mask:
        result.append(mask)
        mask //= 2
    return result


def gather_xor(own):
    pieces = {0: own}
    for mask in masks_of(lax.axis_size("tensor")):
        for j in list(pieces):
            pieces[j | mask] = exchange(pieces[j], "tensor", mask)
    return [pieces[j] for j in range(len(pieces))]


class Sizes:
    def __init__(self, tokens, lengths, qkv_weight, groups, tensors):
        self.bins, self.rows, self.width = tokens.shape
        self.slots = lengths.shape[-1]
        self.buckets = lengths.shape[0]
        self.groups = groups
        self.tensors = tensors
        self.count = self.buckets // groups
        self.moved = self.bins - self.count
        self.heads, self.kinds, self.size = qkv_weight.shape[1:]
        self.depth = self.heads * self.size
        self.order = FIRST
        self.own = self.order + self.count
        self.sent = self.own + self.count
        self.ends = self.sent + self.moved + 1
        self.length = self.ends + self.count * self.slots


def book_kernel(z, ids, source, lengths, tokens, meta, *rest):
    outgoing, sems = rest[:-1], rest[-1]
    group = ids[0]
    for i in range(z.length):
        meta[i] = jnp.int32(0)
    sent = jnp.int32(0)
    partner = jnp.int32(0)
    for b in range(z.buckets):
        owner = b // z.count
        place = source[b] - group * z.bins
        here = (place >= 0) & (place < z.bins) & (owner != group)
        meta[z.sent + jnp.where(here, jnp.minimum(sent, z.moved), z.moved)] = jnp.where(
            here, place, 0
        )
        sent = sent + here.astype(jnp.int32)
        partner = jnp.where(here, owner, partner)
    copies = []
    for m in range(z.moved):
        copies.append(
            pltpu.make_async_copy(tokens.at[meta[z.sent + m]], outgoing[m], sems.at[m])
        )
        copies[-1].start()
    leaving = []
    for m in range(z.count):
        place = source[group * z.count + m] - group * z.bins
        leaving.append(((place < 0) | (place >= z.bins)).astype(jnp.int32))
    left_total = functools.reduce(lambda a, b: a + b, leaving)
    kept_before = jnp.int32(0)
    left_before = z.count - left_total
    for m in range(z.count):
        bucket = group * z.count + m
        leaves = leaving[m] == 1
        place = jnp.where(leaves, left_before, kept_before)
        meta[z.order + place] = jnp.int32(m)
        meta[z.own + place] = jnp.where(leaves, 0, source[bucket] - group * z.bins)
        partner = jnp.where(leaves, lax.div(source[bucket], jnp.int32(z.bins)), partner)
        end = jnp.int32(0)
        for k in range(z.slots):
            end = end + lengths[bucket, k]
            meta[z.ends + place * z.slots + k] = end
        kept_before = kept_before + (1 - leaving[m])
        left_before = left_before + leaving[m]
    receives = left_total > 0
    apart = group ^ partner
    top = jnp.int32(1)
    for k in range(1, z.groups):
        top = jnp.where(apart == k, 1 << (k.bit_length() - 1), top)
    sender = jnp.where(receives, partner, group)
    down = ((sender & top) != 0).astype(jnp.int32)
    meta[CHOSEN] = 2 * jnp.maximum(apart - 1, 0) + down
    meta[RECEIVES] = receives.astype(jnp.int32)
    for i in range(3):
        meta[GROUP + i] = ids[i]
    for copy in copies:
        copy.wait()


def book(z, ids, source_bin, lengths, tokens):
    block = jax.ShapeDtypeStruct((z.rows, z.width), tokens.dtype)
    return pl.pallas_call(
        functools.partial(book_kernel, z),
        out_shape=[jax.ShapeDtypeStruct((z.length,), jnp.int32)] + [block] * z.moved,
        in_specs=[SMEM, SMEM, SMEM, ANY],
        out_specs=[SMEM] + [ANY] * z.moved,
        scratch_shapes=[pltpu.SemaphoreType.DMA((z.moved,))],
        name="book",
    )(ids, source_bin, lengths, tokens)


def norm_kernel(z, m, after, meta, tokens, *rest):
    incoming = rest[0] if m >= z.count - z.moved else None
    rest = rest[(0 if incoming is None else 1) :]
    gain, bias = rest[:2]
    normed, block, sem = rest[2 + after :]
    own = pltpu.make_async_copy(tokens.at[meta[z.own + m]], block, sem)
    if incoming is None:
        own.start()
        own.wait()
    else:
        other = pltpu.make_async_copy(incoming, block, sem)

        @pl.when(meta[RECEIVES] == 1)
        def _():
            other.start()
            other.wait()

        @pl.when(meta[RECEIVES] != 1)
        def _():
            own.start()
            own.wait()

    step = 16

    def rows(i, carry):
        at = pl.ds(pl.multiple_of(i * step, step), step)
        widened = block[at, :].astype(jnp.float32)
        average = jnp.mean(widened, axis=-1, keepdims=True)
        centred = widened - average
        spread = jnp.mean(centred * centred, axis=-1, keepdims=True)
        scaled = centred * lax.rsqrt(spread + 1e-05) * gain[...] + bias[...]
        normed[at, :] = scaled.astype(normed.dtype)
        return carry

    lax.fori_loop(0, z.rows // step, rows, 0)


def normalise(z, m, meta, tokens, incoming, gain, bias, after=()):
    sources = [] if incoming is None else [incoming]
    return pl.pallas_call(
        functools.partial(norm_kernel, z, m, len(after)),
        out_shape=jax.ShapeDtypeStruct((z.rows, z.width), tokens.dtype),
        in_specs=[SMEM, ANY] + [ANY] * len(sources) + [VMEM, VMEM] + [ANY] * len(after),
        out_specs=VMEM,
        scratch_shapes=[
            pltpu.VMEM((z.rows, z.width), tokens.dtype),
            pltpu.SemaphoreType.DMA,
        ],
        compiler_params=pltpu.CompilerParams(vmem_limit_bytes=16 * MIB),
        name="normalise",
    )(meta, tokens, *sources, gain, bias, *after)


def slot_rows(z, meta, shape, axis):
    index = lax.broadcasted_iota(jnp.int32, shape, axis)
    piece = lax.div(index, jnp.int32(z.rows))
    return (meta[RANK] ^ piece) * z.rows + (index - piece * z.rows)


def members(z, meta, m, rows):
    member = jnp.zeros(rows.shape, jnp.int32)
    for k in range(z.slots):
        member = member + (rows >= meta[z.ends + m * z.slots + k]).astype(jnp.int32)
    return member


def table_kernel(z, m, after, meta, *rest):
    cosine, sine = rest[after:]
    full = z.rows * z.tensors
    rows = slot_rows(z, meta, (full, 1), 0)
    member = members(z, meta, m, rows)
    start = jnp.zeros(rows.shape, jnp.int32)
    for k in range(1, z.slots):
        start = jnp.where(member == k, meta[z.ends + m * z.slots + k - 1], start)
    position = (rows - start).astype(jnp.float32)
    lane = lax.broadcasted_iota(jnp.int32, (1, z.size), 1)
    half = z.size // 2
    index = jnp.where(lane < half, lane, lane - half).astype(jnp.float32)
    frequency = jnp.exp(index * jnp.float32(-2.0 / z.size * 9.210340371976184))
    angle = position * frequency
    cosine[...] = jnp.cos(angle)
    turned = jnp.sin(angle)
    sine[...] = jnp.where(lane < half, -turned, turned)


def tables(z, m, meta, after=()):
    shape = jax.ShapeDtypeStruct((z.rows * z.tensors, z.size), jnp.float32)
    return pl.pallas_call(
        functools.partial(table_kernel, z, m, len(after)),
        out_shape=[shape, shape],
        in_specs=[SMEM] + [ANY] * len(after),
        out_specs=[VMEM, VMEM],
        name="tables",
    )(meta, *after)


def attend_kernel(z, m, steps, swaps, meta, *rest):
    n = z.tensors
    pieces = rest[:n]
    weight, bias, cosine, sine = rest[n : n + 4]
    outputs = rest[n + 4 : n + 4 + n]
    rows, total = rest[n + 4 + n :]
    step = pl.program_id(0)
    for j in range(n):
        rows[j * z.rows : (j + 1) * z.rows, :] = pieces[j][...]
    product = jnp.dot(rows[...], weight[...], preferred_element_type=jnp.float32)

    @pl.when(step == 0)
    def _():
        total[...] = product + bias[...]

    @pl.when(step != 0)
    def _():
        total[...] += product

    @pl.when(step == steps - 1)
    def _():
        full = n * z.rows
        row_member = members(z, meta, m, slot_rows(z, meta, (full, 1), 0))
        column_member = members(z, meta, m, slot_rows(z, meta, (1, full), 1))
        allowed = (row_member == column_member) & (column_member < z.slots)
        cos, sin = cosine[...], sine[...]

        def turn(u):
            return (u * cos + pltpu.roll(u, z.size // 2, 1) * sin).astype(jnp.bfloat16)

        contexts = []
        for h in range(z.heads):
            at = [slice((k * z.heads + h) * z.size, (k * z.heads + h + 1) * z.size) for k in range(3)]
            queries = turn(total[:, at[0]] * jnp.float32(z.size ** (-0.5)))
            key_rows = turn(total[:, at[1]])
            values = total[:, at[2]].astype(jnp.bfloat16)
            scores = lax.dot_general(
                queries, key_rows, (((1,), (1,)), ((), ())), preferred_element_type=jnp.float32
            )
            masked = jnp.where(allowed, scores, jnp.float32(-1e30))
            raised = jnp.exp(masked - jnp.max(masked, axis=-1, keepdims=True))
            share = raised / jnp.sum(raised, axis=-1, keepdims=True)
            context = jnp.dot(
                share.astype(jnp.bfloat16), values, preferred_element_type=jnp.float32
            )
            contexts.append(context)
        plain = jnp.concatenate(contexts, axis=-1)
        half = z.depth // 2
        turned = jnp.concatenate([plain[:, half:], plain[:, :half]], axis=-1)
        if swaps:
            turned = jnp.where(meta[PART] == 1, turned, plain)
        else:
            turned = plain
        for j in range(n):
            value = (turned if j > 1 else plain)[j * z.rows : (j + 1) * z.rows]
            outputs[j][...] = value.astype(jnp.bfloat16)


def attend(z, m, meta, pieces, weight, bias, table, swaps):
    steps = 4
    chunk = z.width // steps
    columns = z.kinds * z.depth
    full = z.rows * z.tensors
    whole = pl.BlockSpec((full, z.size), lambda i, s: (0, 0))
    return pl.pallas_call(
        functools.partial(attend_kernel, z, m, steps, swaps),
        out_shape=[jax.ShapeDtypeStruct((z.rows, z.depth), jnp.bfloat16)] * z.tensors,
        grid_spec=pltpu.PrefetchScalarGridSpec(
            num_scalar_prefetch=1,
            grid=(steps,),
            in_specs=[pl.BlockSpec((z.rows, chunk), lambda i, s: (0, i))] * z.tensors
            + [
                pl.BlockSpec((chunk, columns), lambda i, s: (i, 0)),
                pl.BlockSpec((1, columns), lambda i, s: (0, 0)),
                whole,
                whole,
            ],
            out_specs=[pl.BlockSpec((z.rows, z.depth), lambda i, s: (0, 0))] * z.tensors,
            scratch_shapes=[
                pltpu.VMEM((full, chunk), jnp.bfloat16),
                pltpu.VMEM((full, columns), jnp.float32),
            ],
        ),
        compiler_params=pltpu.CompilerParams(vmem_limit_bytes=24 * MIB),
        name="attend",
    )(meta, *pieces, weight, bias, *table)


def output_kernel(z, depths, meta, *rest):
    contexts = rest[: z.count * z.tensors]
    rest = rest[z.count * z.tensors :]
    weights = rest[: len(depths)]
    rest = rest[len(depths) :]
    own, rest = rest[: z.count], rest[z.count :]
    incoming, rest = rest[: z.moved], rest[z.moved :]
    bias, out, joined = rest
    for m in range(z.count):
        for j in range(z.tensors):
            joined[m * z.rows : (m + 1) * z.rows, j * z.depth : (j + 1) * z.depth] = contexts[
                m * z.tensors + j
            ][...]
    total = None
    place = 0
    for weight, depth in zip(weights, depths):
        term = jnp.dot(
            joined[:, place : place + depth], weight[...], preferred_element_type=jnp.float32
        )
        total = term if total is None else total + term
        place += depth
    index = meta[RANK] * z.rows + lax.broadcasted_iota(jnp.int32, (z.rows, 1), 0)
    for m in range(z.count):
        block = own[m][0]
        k = m - (z.count - z.moved)
        if k >= 0:
            block = jnp.where(meta[RECEIVES] == 1, incoming[k][...], block)
        value = block.astype(jnp.float32) + total[m * z.rows : (m + 1) * z.rows] + bias[...]
        held = index < meta[z.ends + m * z.slots + z.slots - 1]
        out[meta[z.order + m]] = jnp.where(held, value, jnp.float32(0.0)).astype(out.dtype)


def project(z, meta, contexts, weights, tokens, incoming, bias):
    steps = 10
    chunk = z.width // steps
    depths = [w.shape[0] for w in weights]
    flat = [c for bucket in contexts for c in bucket]
    own_specs = [
        pl.BlockSpec((1, z.rows, chunk), functools.partial(lambda m, i, s: (s[z.own + m], 0, i), m))
        for m in range(z.count)
    ]
    return pl.pallas_call(
        functools.partial(output_kernel, z, depths),
        out_shape=jax.ShapeDtypeStruct((z.count, z.rows, z.width), tokens.dtype),
        grid_spec=pltpu.PrefetchScalarGridSpec(
            num_scalar_prefetch=1,
            grid=(steps,),
            in_specs=[pl.BlockSpec((z.rows, z.depth), lambda i, s: (0, 0))] * len(flat)
            + [pl.BlockSpec((depth, chunk), lambda i, s: (0, i)) for depth in depths]
            + own_specs
            + [pl.BlockSpec((z.rows, chunk), lambda i, s: (0, i))] * z.moved
            + [pl.BlockSpec((1, chunk), lambda i, s: (0, i))],
            out_specs=pl.BlockSpec((z.count, z.rows, chunk), lambda i, s: (0, 0, i)),
            scratch_shapes=[pltpu.VMEM((z.count * z.rows, z.tensors * z.depth), jnp.bfloat16)],
        ),
        compiler_params=pltpu.CompilerParams(vmem_limit_bytes=32 * MIB),
        name="project",
    )(meta, *flat, *weights, *([tokens] * z.count), *incoming, bias)


def on_device(
    tokens, norm_gain, norm_bias, qkv_weight, qkv_bias, out_weight, out_bias, lengths, source_bin
):
    groups = lax.axis_size("dp")
    tensors = lax.axis_size("tensor")
    z = Sizes(tokens, lengths, qkv_weight, groups, tensors)
    part = lax.axis_index("parts")
    ids = jnp.stack([lax.axis_index("dp"), lax.axis_index("tensor"), part]).astype(jnp.int32)
    meta, *outgoing = book(z, ids, source_bin, lengths, tokens)

    gain, bias = norm_gain.reshape(1, -1), norm_bias.reshape(1, -1)
    qkv_row = jnp.transpose(qkv_bias, (1, 0, 2)).reshape(1, -1)
    flat_out = out_weight.reshape(z.depth, z.width)
    split = lax.axis_size("parts") == 2 and tensors > 2
    kept = z.count - z.moved
    small = tensors <= 4

    def send_back(contexts):
        return [contexts[0]] + [exchange(contexts[j], "tensor", j) for j in range(1, tensors)]

    def relayout(weight):
        return jnp.transpose(weight, (0, 2, 1, 3)).reshape(z.width, z.kinds * z.depth)

    def out_firsts(after):
        first = flat_out
        if split:
            half = z.depth // 2
            first = lax.dynamic_slice_in_dim(flat_out, part * half, half, 0)
        firsts = {0: first}
        for mask in masks_of(tensors)[:-1]:
            for j in list(firsts):
                firsts[j | mask] = exchange(firsts[j], "tensor", mask)
        del firsts[0]
        return firsts

    def work(m, pieces, weight, after):
        return send_back(
            attend(z, m, meta, pieces, weight, qkv_row, tables(z, m, meta, after), split)
        )

    def start(m, incoming, after=()):
        k = m - kept
        source = incoming[k] if k >= 0 else None
        return gather_xor(normalise(z, m, meta, tokens, source, gain, bias, after))

    def branch(pairs):
        def run():
            incoming = [lax.ppermute(block, "dp", pairs) for block in outgoing]
            if not small:
                return (incoming,)
            pieces = start(0, incoming)
            raw, _ = lax.optimization_barrier((qkv_weight, pieces[0]))
            weight = relayout(raw)
            firsts = out_firsts(pieces[0])
            contexts = [work(0, pieces, weight, (weight,))]
            for m in range(1, z.count - 1):
                pieces = start(m, incoming, (contexts[-1][0],))
            return incoming, weight, firsts, contexts, pieces

        return run

    branches = []
    for k in range(1, groups):
        top = 1 << (k.bit_length() - 1)
        up = [(i, i ^ k) for i in range(groups) if not i & top]
        branches.append(branch(up))
        branches.append(branch([(d, s) for s, d in up]))
    result = lax.switch(meta[CHOSEN], branches)
    if small:
        incoming, weight, firsts, contexts, held = result
        last = start(z.count - 1, incoming)
        contexts.append(work(z.count - 2, held, weight, (last[0],)))
        contexts.append(work(z.count - 1, last, weight, (last[0],)))
    else:
        (incoming,) = result
        weight = relayout(qkv_weight)
        firsts = out_firsts(incoming[0])
        contexts = [work(m, start(m, incoming), weight, ()) for m in range(z.count)]

    rows_of = {0: [flat_out]}
    if tensors > 1:
        rows_of[1] = [exchange(flat_out, "tensor", 1)]
    for j in firsts:
        held = [firsts[j]]
        if split:
            held.append(exchange(firsts[j], "parts", 1))
        rows_of[j] = held
        rows_of[j | 1] = [exchange(h, "tensor", 1) for h in held]
    weights = [h for j in range(tensors) for h in rows_of[j]]
    return project(z, meta, contexts, weights, tokens, incoming, out_bias.reshape(1, -1))


def solution(mesh):
    return jax.shard_map(
        on_device,
        mesh=mesh,
        in_specs=(
            P(("parts", "dp"), "tensor", None),
            P(),
            P(),
            P(None, "tensor", None, None),
            P("tensor", None, None),
            P("tensor", None, None),
            P(),
            P("parts", None),
            P("parts"),
        ),
        out_specs=P(("parts", "dp"), "tensor", None),
        check_vma=False,
    )
```

```python
import functools

import jax
import jax.numpy as jnp
from jax import lax
from jax.experimental import pallas as pl
from jax.experimental.pallas import tpu as pltpu
from jax.sharding import PartitionSpec as P

MIB = 1 << 20
COST = pl.CostEstimate(flops=0, bytes_accessed=0, transcendentals=0)
CHOSEN, RECEIVES, GROUP, RANK, PART, FIRST = 0, 1, 2, 3, 4, 8
ANY = pl.BlockSpec(memory_space=pl.ANY)
SMEM = pl.BlockSpec(memory_space=pltpu.SMEM)
VMEM = pl.BlockSpec(memory_space=pltpu.VMEM)


def exchange(value, axis, mask):
    size = lax.axis_size(axis)
    return lax.ppermute(value, axis, [(i, i ^ mask) for i in range(size)])


def masks_of(size):
    mask = size // 2
    result = []
    while mask:
        result.append(mask)
        mask //= 2
    return result


def gather_xor(own, after=None):
    pieces = {0: own}
    for mask in masks_of(lax.axis_size("tensor")):
        for j in list(pieces):
            piece = pieces[j]
            if j and after is not None:
                piece, _ = lax.optimization_barrier((piece, after()))
            pieces[j | mask] = exchange(piece, "tensor", mask)
    return [pieces[j] for j in range(len(pieces))]


class Sizes:
    def __init__(self, tokens, lengths, qkv_weight, groups, tensors):
        self.bins, self.rows, self.width = tokens.shape
        self.slots = lengths.shape[-1]
        self.buckets = lengths.shape[0]
        self.groups = groups
        self.tensors = tensors
        self.count = self.buckets // groups
        self.moved = self.bins - self.count
        self.heads, self.kinds, self.size = qkv_weight.shape[1:]
        self.depth = self.heads * self.size
        self.order = FIRST
        self.own = self.order + self.count
        self.sent = self.own + self.count
        self.ends = self.sent + self.moved + 1
        self.length = self.ends + self.count * self.slots


def book_kernel(z, source, lengths, tokens, out_weight, meta, *rest):
    outgoing, first, sems = rest[:-2], rest[-2], rest[-1]
    ids = [lax.axis_index(axis) for axis in ("dp", "tensor", "parts")]
    group = ids[0]
    deep = first.shape[0]
    copies = [
        pltpu.make_async_copy(
            out_weight.at[pl.ds(pl.multiple_of(ids[2] * deep, deep), deep)],
            first,
            sems.at[z.moved],
        )
    ]
    copies[0].start()
    for i in range(z.length):
        meta[i] = jnp.int32(0)
    sent = jnp.int32(0)
    partner = jnp.int32(0)
    for b in range(z.buckets):
        owner = b // z.count
        place = source[b] - group * z.bins
        here = (place >= 0) & (place < z.bins) & (owner != group)
        meta[z.sent + jnp.where(here, jnp.minimum(sent, z.moved), z.moved)] = jnp.where(
            here, place, 0
        )
        sent = sent + here.astype(jnp.int32)
        partner = jnp.where(here, owner, partner)
    for m in range(z.moved):
        copies.append(
            pltpu.make_async_copy(tokens.at[meta[z.sent + m]], outgoing[m], sems.at[m])
        )
        copies[-1].start()
    leaving = []
    for m in range(z.count):
        place = source[group * z.count + m] - group * z.bins
        leaving.append(((place < 0) | (place >= z.bins)).astype(jnp.int32))
    left_total = functools.reduce(lambda a, b: a + b, leaving)
    kept_before = jnp.int32(0)
    left_before = z.count - left_total
    for m in range(z.count):
        bucket = group * z.count + m
        leaves = leaving[m] == 1
        place = jnp.where(leaves, left_before, kept_before)
        meta[z.order + place] = jnp.int32(m)
        meta[z.own + place] = jnp.where(leaves, 0, source[bucket] - group * z.bins)
        partner = jnp.where(leaves, lax.div(source[bucket], jnp.int32(z.bins)), partner)
        end = jnp.int32(0)
        for k in range(z.slots):
            end = end + lengths[k, bucket]
            meta[z.ends + place * z.slots + k] = end
        kept_before = kept_before + (1 - leaving[m])
        left_before = left_before + leaving[m]
    receives = left_total > 0
    apart = group ^ partner
    top = jnp.int32(1)
    for k in range(1, z.groups):
        top = jnp.where(apart == k, 1 << (k.bit_length() - 1), top)
    sender = jnp.where(receives, partner, group)
    down = ((sender & top) != 0).astype(jnp.int32)
    meta[CHOSEN] = 2 * jnp.maximum(apart - 1, 0) + down
    meta[RECEIVES] = receives.astype(jnp.int32)
    for i in range(3):
        meta[GROUP + i] = ids[i]
    for copy in copies:
        copy.wait()


def book(z, source_bin, lengths, tokens, flat_out):
    block = jax.ShapeDtypeStruct((z.rows, z.width), tokens.dtype)
    first = jax.ShapeDtypeStruct((z.depth // 2, z.width), flat_out.dtype)
    return pl.pallas_call(
        functools.partial(book_kernel, z),
        out_shape=[jax.ShapeDtypeStruct((z.length,), jnp.int32)] + [block] * z.moved + [first],
        in_specs=[SMEM, SMEM, ANY, ANY],
        out_specs=[SMEM] + [VMEM] * (z.moved + 1),
        scratch_shapes=[pltpu.SemaphoreType.DMA((z.moved + 1,))],
        compiler_params=pltpu.CompilerParams(vmem_limit_bytes=16 * MIB),
        cost_estimate=COST,
        name="book",
    )(source_bin, lengths.T, tokens, flat_out)


def norm_kernel(z, m, after, meta, tokens, *rest):
    incoming = rest[0] if m >= z.count - z.moved else None
    rest = rest[(0 if incoming is None else 1) :]
    gain, bias = rest[:2]
    normed, block, sem = rest[2 + after :]
    own = pltpu.make_async_copy(tokens.at[meta[z.own + m]], block, sem)
    if incoming is None:
        own.start()
        own.wait()
    else:
        other = pltpu.make_async_copy(incoming, block, sem)

        @pl.when(meta[RECEIVES] == 1)
        def _():
            other.start()
            other.wait()

        @pl.when(meta[RECEIVES] != 1)
        def _():
            own.start()
            own.wait()

    step = 16

    def rows(i, carry):
        at = pl.ds(pl.multiple_of(i * step, step), step)
        widened = block[at, :].astype(jnp.float32)
        average = jnp.mean(widened, axis=-1, keepdims=True)
        centred = widened - average
        spread = jnp.mean(centred * centred, axis=-1, keepdims=True)
        scaled = centred * lax.rsqrt(spread + 1e-05) * gain[...] + bias[...]
        normed[at, :] = scaled.astype(normed.dtype)
        return carry

    lax.fori_loop(0, z.rows // step, rows, 0, unroll=True)


def normalise(z, m, meta, tokens, incoming, gain, bias, after=()):
    sources = [] if incoming is None else [incoming]
    return pl.pallas_call(
        functools.partial(norm_kernel, z, m, len(after)),
        out_shape=jax.ShapeDtypeStruct((z.rows, z.width), tokens.dtype),
        in_specs=[SMEM, ANY] + [ANY] * len(sources) + [VMEM, VMEM] + [ANY] * len(after),
        out_specs=VMEM,
        scratch_shapes=[
            pltpu.VMEM((z.rows, z.width), tokens.dtype),
            pltpu.SemaphoreType.DMA,
        ],
        compiler_params=pltpu.CompilerParams(vmem_limit_bytes=16 * MIB),
        cost_estimate=COST,
        name="normalise",
    )(meta, tokens, *sources, gain, bias, *after)


def slot_rows(z, meta, shape, axis):
    index = lax.broadcasted_iota(jnp.int32, shape, axis)
    piece = lax.div(index, jnp.int32(z.rows))
    return (meta[RANK] ^ piece) * z.rows + (index - piece * z.rows)


def members(z, meta, m, rows):
    member = jnp.zeros(rows.shape, jnp.int32)
    for k in range(z.slots):
        member = member + (rows >= meta[z.ends + m * z.slots + k]).astype(jnp.int32)
    return member


def tables(z, meta, m, rows, member):
    start = jnp.zeros(rows.shape, jnp.int32)
    for k in range(1, z.slots):
        start = jnp.where(member == k, meta[z.ends + m * z.slots + k - 1], start)
    position = (rows - start).astype(jnp.float32)
    lane = lax.broadcasted_iota(jnp.int32, (1, z.size), 1)
    half = z.size // 2
    index = jnp.where(lane < half, lane, lane - half).astype(jnp.float32)
    frequency = jnp.exp(index * jnp.float32(-2.0 / z.size * 9.210340371976184))
    angle = position * frequency
    turned = jnp.sin(angle)
    return jnp.cos(angle), jnp.where(lane < half, -turned, turned)


def attend_kernel(z, buckets, steps, swaps, after, meta, *rest):
    n, count = z.tensors, len(buckets)
    pieces, rest = rest[: n * count], rest[n * count :]
    weight, bias = rest[:2]
    rest = rest[2 + after :]
    outputs, rest = rest[:n], rest[n:]
    rows, held, total, cosine, sine, sems = rest
    full = n * z.rows
    chunk = z.width // steps
    columns = z.kinds * z.depth
    fetches = []
    for s in range(steps):
        at = slice(s * chunk, (s + 1) * chunk)
        now = [pltpu.make_async_copy(weight.at[at], held.at[at], sems.at[s, 0])]
        for i in range(n * count):
            now.append(
                pltpu.make_async_copy(
                    pieces[i].at[:, at],
                    rows.at[i * z.rows : (i + 1) * z.rows, at],
                    sems.at[s, i + 1],
                )
            )
        for copy in now:
            copy.start()
        fetches.append(now)
    for i, m in enumerate(buckets):
        index = slot_rows(z, meta, (full, 1), 0)
        cosine[i], sine[i] = tables(z, meta, m, index, members(z, meta, m, index))
    for s in range(steps):
        at = slice(s * chunk, (s + 1) * chunk)
        for copy in fetches[s]:
            copy.wait()
        product = jnp.dot(rows[:, at], held[at, :], preferred_element_type=jnp.float32)
        if s == 0:
            total[...] = product + bias[...]
        else:
            total[...] += product
    for i, m in enumerate(buckets):
        row_member = members(z, meta, m, slot_rows(z, meta, (full, 1), 0))
        column_member = members(z, meta, m, slot_rows(z, meta, (1, full), 1))
        allowed = (row_member == column_member) & (column_member < z.slots)
        cos, sin = cosine[i], sine[i]

        def turn(u):
            return (u * cos + pltpu.roll(u, z.size // 2, 1) * sin).astype(jnp.bfloat16)

        def part(kind, h):
            place = (kind * z.heads + h) * z.size
            return total[i * full : (i + 1) * full, place : place + z.size]

        contexts = []
        for h in range(z.heads):
            queries = turn(part(0, h) * jnp.float32(z.size ** (-0.5)))
            key_rows = turn(part(1, h))
            values = part(2, h).astype(jnp.bfloat16)
            scores = lax.dot_general(
                queries, key_rows, (((1,), (1,)), ((), ())), preferred_element_type=jnp.float32
            )
            masked = jnp.where(allowed, scores, jnp.float32(-1e30))
            raised = jnp.exp(masked - jnp.max(masked, axis=-1, keepdims=True))
            share = raised / jnp.sum(raised, axis=-1, keepdims=True)
            contexts.append(
                jnp.dot(share.astype(jnp.bfloat16), values, preferred_element_type=jnp.float32)
            )
        plain = jnp.concatenate(contexts, axis=-1)
        half = z.depth // 2
        turned = plain
        if swaps:
            turned = jnp.concatenate([plain[:, half:], plain[:, :half]], axis=-1)
            turned = jnp.where(meta[PART] == 1, turned, plain)
        for j in range(n):
            value = (turned if j > 1 else plain)[j * z.rows : (j + 1) * z.rows]
            outputs[j][i * z.rows : (i + 1) * z.rows, :] = value.astype(jnp.bfloat16)


def attend(z, buckets, meta, pieces, weight, bias, swaps, after=()):
    steps = 5
    count = len(buckets)
    columns = z.kinds * z.depth
    full = z.rows * z.tensors
    flat = [p for bucket in pieces for p in bucket]
    return pl.pallas_call(
        functools.partial(attend_kernel, z, buckets, steps, swaps, len(after)),
        out_shape=[jax.ShapeDtypeStruct((count * z.rows, z.depth), jnp.bfloat16)] * z.tensors,
        in_specs=[SMEM] + [ANY] * len(flat) + [ANY, VMEM] + [ANY] * len(after),
        out_specs=[VMEM] * z.tensors,
        scratch_shapes=[
            pltpu.VMEM((count * full, z.width), jnp.bfloat16),
            pltpu.VMEM((z.width, columns), jnp.bfloat16),
            pltpu.VMEM((count * full, columns), jnp.float32),
            pltpu.VMEM((count, full, z.size), jnp.float32),
            pltpu.VMEM((count, full, z.size), jnp.float32),
            pltpu.SemaphoreType.DMA((steps, len(flat) + 1)),
        ],
        compiler_params=pltpu.CompilerParams(vmem_limit_bytes=60 * MIB),
        cost_estimate=pl.CostEstimate(
            flops=2 * count * full * z.width * columns,
            bytes_accessed=2 * z.width * (count * full + columns),
            transcendentals=count * z.heads * full * full,
        ),
        name="attend",
    )(meta, *flat, weight, bias, *after)


def output_kernel(z, depths, counts, steps, meta, *rest):
    contexts, rest = rest[: len(counts) * z.tensors], rest[len(counts) * z.tensors :]
    weights, rest = rest[: len(depths)], rest[len(depths) :]
    tokens, incoming, bias, out = rest[0], rest[1 : 1 + z.moved], rest[1 + z.moved], rest[2 + z.moved]
    held, blocks, joined, ready, sems, block_sems, out_sems = rest[3 + z.moved :]
    chunk = z.width // steps
    fetches = []
    for s in range(steps):
        at = slice(s * chunk, (s + 1) * chunk)
        now = []
        place = 0
        for i, depth in enumerate(depths):
            now.append(
                pltpu.make_async_copy(
                    weights[i].at[:, at], held.at[place : place + depth, at], sems.at[s, i]
                )
            )
            now[-1].start()
            place += depth
        fetches.append(now)
        if s == 0:
            own = [
                pltpu.make_async_copy(
                    tokens.at[meta[z.own + m]], blocks.at[m], block_sems.at[m]
                )
                for m in range(z.count)
            ]
            kept = z.count - z.moved
            other = [
                pltpu.make_async_copy(incoming[k], blocks.at[kept + k], block_sems.at[kept + k])
                for k in range(z.moved)
            ]
            for m in range(kept):
                own[m].start()

            @pl.when(meta[RECEIVES] == 1)
            def _():
                for copy in other:
                    copy.start()

            @pl.when(meta[RECEIVES] != 1)
            def _():
                for copy in own[kept:]:
                    copy.start()

    m = 0
    for g, count in enumerate(counts):
        for j in range(z.tensors):
            joined[m * z.rows : (m + count) * z.rows, j * z.depth : (j + 1) * z.depth] = contexts[
                g * z.tensors + j
            ][...]
        m += count
    index = meta[RANK] * z.rows + lax.broadcasted_iota(jnp.int32, (z.rows, 1), 0)
    leaving = []
    for s in range(steps):
        at = slice(s * chunk, (s + 1) * chunk)
        for copy in fetches[s]:
            copy.wait()
        total = jnp.dot(joined[...], held[:, at], preferred_element_type=jnp.float32)
        if s == 0:
            for copy in own:
                copy.wait()
        for m in range(z.count):
            block = blocks[m, :, at].astype(jnp.float32)
            value = block + total[m * z.rows : (m + 1) * z.rows] + bias[:, at]
            there = index < meta[z.ends + m * z.slots + z.slots - 1]
            ready[m, :, at] = jnp.where(there, value, jnp.float32(0.0)).astype(out.dtype)
            copy = pltpu.make_async_copy(
                ready.at[m, :, at], out.at[meta[z.order + m], :, at], out_sems.at[s, m]
            )
            copy.start()
            leaving.append(copy)
    for copy in leaving:
        copy.wait()


def project(z, meta, contexts, counts, weights, tokens, incoming, bias):
    steps = 5
    depths = [w.shape[0] for w in weights]
    flat = [c for bucket in contexts for c in bucket]
    return pl.pallas_call(
        functools.partial(output_kernel, z, depths, counts, steps),
        out_shape=jax.ShapeDtypeStruct((z.count, z.rows, z.width), tokens.dtype),
        in_specs=[SMEM]
        + [VMEM] * len(flat)
        + [ANY] * len(depths)
        + [ANY]
        + [ANY] * z.moved
        + [VMEM],
        out_specs=ANY,
        scratch_shapes=[
            pltpu.VMEM((sum(depths), z.width), jnp.bfloat16),
            pltpu.VMEM((z.count, z.rows, z.width), tokens.dtype),
            pltpu.VMEM((z.count * z.rows, z.tensors * z.depth), jnp.bfloat16),
            pltpu.VMEM((z.count, z.rows, z.width), tokens.dtype),
            pltpu.SemaphoreType.DMA((steps, len(depths))),
            pltpu.SemaphoreType.DMA((z.count,)),
            pltpu.SemaphoreType.DMA((steps, z.count)),
        ],
        compiler_params=pltpu.CompilerParams(vmem_limit_bytes=60 * MIB),
        cost_estimate=COST,
        name="project",
    )(meta, *flat, *weights, tokens, *incoming, bias)


def on_device(
    tokens, norm_gain, norm_bias, qkv_weight, qkv_bias, out_weight, out_bias, lengths, source_bin
):
    groups = lax.axis_size("dp")
    tensors = lax.axis_size("tensor")
    z = Sizes(tokens, lengths, qkv_weight, groups, tensors)
    flat_out = out_weight.reshape(z.depth, z.width)
    meta, *outgoing, half_out = book(z, source_bin, lengths, tokens, flat_out)

    gain, bias = norm_gain.reshape(1, -1), norm_bias.reshape(1, -1)
    qkv_row = jnp.transpose(qkv_bias, (1, 0, 2)).reshape(1, -1)
    split = lax.axis_size("parts") == 2 and tensors > 2
    kept = z.count - z.moved
    small = tensors <= 4

    def send_back(contexts):
        return [contexts[0]] + [exchange(contexts[j], "tensor", j) for j in range(1, tensors)]

    def relayout(weight):
        return jnp.transpose(weight, (0, 2, 1, 3)).reshape(z.width, z.kinds * z.depth)

    def out_firsts():
        firsts = {0: half_out if split else flat_out}
        for mask in masks_of(tensors)[:-1]:
            for j in list(firsts):
                firsts[j | mask] = exchange(firsts[j], "tensor", mask)
        del firsts[0]
        return firsts

    def work(buckets, pieces, weight):
        return attend(z, buckets, meta, pieces, weight, qkv_row, split)

    def start(m, incoming, after=()):
        source = incoming[m - kept] if m >= kept else None
        return normalise(z, m, meta, tokens, source, gain, bias, after)

    ways = []
    for k in range(1, groups):
        top = 1 << (k.bit_length() - 1)
        up = [(i, i ^ k) for i in range(groups) if not i & top]
        ways += [up, [(d, s) for s, d in up]]

    def choose(branch):
        return lax.switch(meta[CHOSEN], [functools.partial(branch, pairs) for pairs in ways])

    last = z.count - 1
    if small:

        def early(pairs):
            arrived = [lax.ppermute(block, "dp", pairs) for block in outgoing[:-1]]
            firsts = out_firsts()
            weight = relayout(qkv_weight)
            return arrived, firsts, weight, start(0, arrived, (weight,))

        arrived, firsts, weight, normed = choose(early)

        def late(pairs):
            arriving = lax.ppermute(outgoing[-1], "dp", pairs)
            held = [gather_xor(normed)]
            for m in range(1, last):
                held.append(gather_xor(start(m, arrived)))
            return arriving, held

        arriving, held = choose(late)
        incoming = arrived + [arriving]
        normed = start(last, incoming)
        counts = [last, 1]
        contexts = [send_back(work(list(range(last)), held, weight))]
        pieces = gather_xor(normed, lambda: contexts[0][0])
        contexts.append(send_back(work([last], [pieces], weight)))
    else:
        incoming = choose(lambda pairs: [lax.ppermute(b, "dp", pairs) for b in outgoing])
        weight = relayout(qkv_weight)
        firsts = out_firsts()
        counts = [1] * z.count
        contexts = [
            send_back(work([m], [gather_xor(start(m, incoming))], weight))
            for m in range(z.count)
        ]

    rows_of = {0: [flat_out]}
    if tensors > 1:
        rows_of[1] = [exchange(flat_out, "tensor", 1)]
    for j in firsts:
        held = [firsts[j]]
        rows_of[j | 1] = [exchange(firsts[j], "tensor", 1)]
        if split:
            second = exchange(firsts[j], "parts", 1)
            held.append(second)
            second, _ = lax.optimization_barrier((second, contexts[-1][0]))
            rows_of[j | 1].append(exchange(second, "tensor", 1))
        rows_of[j] = held
    weights = [h for j in range(tensors) for h in rows_of[j]]
    return project(z, meta, contexts, counts, weights, tokens, incoming, out_bias.reshape(1, -1))


def solution(mesh):
    return jax.shard_map(
        on_device,
        mesh=mesh,
        in_specs=(
            P(("parts", "dp"), "tensor", None),
            P(),
            P(),
            P(None, "tensor", None, None),
            P("tensor", None, None),
            P("tensor", None, None),
            P(),
            P("parts", None),
            P("parts"),
        ),
        out_specs=P(("parts", "dp"), "tensor", None),
        check_vma=False,
    )
```

```python
import functools

import jax
import jax.numpy as jnp
from jax import lax
from jax.experimental import pallas as pl
from jax.experimental.layout import Layout, with_layout_constraint
from jax.experimental.pallas import tpu as pltpu
from jax.sharding import PartitionSpec as P

MIB = 1 << 20
COST = pl.CostEstimate(flops=0, bytes_accessed=0, transcendentals=0)
CHOSEN, RECEIVES, GROUP, RANK, PART, FIRST = 0, 1, 2, 3, 4, 8
ANY = pl.BlockSpec(memory_space=pl.ANY)
SMEM = pl.BlockSpec(memory_space=pltpu.SMEM)
VMEM = pl.BlockSpec(memory_space=pltpu.VMEM)


def exchange(value, axis, mask):
    size = lax.axis_size(axis)
    return lax.ppermute(value, axis, [(i, i ^ mask) for i in range(size)])


def masks_of(size):
    mask = size // 2
    result = []
    while mask:
        result.append(mask)
        mask //= 2
    return result


def hop(own):
    return exchange(own, "tensor", lax.axis_size("tensor") // 2)


def gather_xor(own, crossed=None, after=None):
    pieces = {0: own}
    for mask in masks_of(lax.axis_size("tensor")):
        for j in list(pieces):
            piece = pieces[j]
            if crossed is not None and len(pieces) == 1:
                pieces[j | mask] = crossed
                continue
            if j and after is not None:
                piece, _ = lax.optimization_barrier((piece, after))
            pieces[j | mask] = exchange(piece, "tensor", mask)
    return [pieces[j] for j in range(len(pieces))]


class Sizes:
    def __init__(self, tokens, lengths, qkv_weight, groups, tensors):
        self.bins, self.rows, self.width = tokens.shape
        self.slots = lengths.shape[-1]
        self.buckets = lengths.shape[0]
        self.groups = groups
        self.tensors = tensors
        self.count = self.buckets // groups
        self.moved = self.bins - self.count
        self.heads, self.kinds, self.size = qkv_weight.shape[1:]
        self.depth = self.heads * self.size
        self.order = FIRST
        self.own = self.order + self.count
        self.sent = self.own + self.count
        self.ends = self.sent + self.moved + 1
        self.length = self.ends + self.count * self.slots


def book_kernel(z, source, lengths, tokens, out_weight, meta, *rest):
    outgoing, first, sems = rest[:-2], rest[-2], rest[-1]
    ids = [lax.axis_index(axis) for axis in ("dp", "tensor", "parts")]
    group = ids[0]
    deep = first.shape[0]
    copies = [
        pltpu.make_async_copy(
            out_weight.at[pl.ds(pl.multiple_of(ids[2] * deep, deep), deep)],
            first,
            sems.at[z.moved],
        )
    ]
    copies[0].start()
    for i in range(z.length):
        meta[i] = jnp.int32(0)
    sent = jnp.int32(0)
    partner = jnp.int32(0)
    for b in range(z.buckets):
        owner = b // z.count
        place = source[b] - group * z.bins
        here = (place >= 0) & (place < z.bins) & (owner != group)
        meta[z.sent + jnp.where(here, jnp.minimum(sent, z.moved), z.moved)] = jnp.where(
            here, place, 0
        )
        sent = sent + here.astype(jnp.int32)
        partner = jnp.where(here, owner, partner)
    for m in range(z.moved):
        copies.append(
            pltpu.make_async_copy(tokens.at[meta[z.sent + m]], outgoing[m], sems.at[m])
        )
        copies[-1].start()
    leaving = []
    for m in range(z.count):
        place = source[group * z.count + m] - group * z.bins
        leaving.append(((place < 0) | (place >= z.bins)).astype(jnp.int32))
    left_total = functools.reduce(lambda a, b: a + b, leaving)
    kept_before = jnp.int32(0)
    left_before = z.count - left_total
    for m in range(z.count):
        bucket = group * z.count + m
        leaves = leaving[m] == 1
        place = jnp.where(leaves, left_before, kept_before)
        meta[z.order + place] = jnp.int32(m)
        meta[z.own + place] = jnp.where(leaves, 0, source[bucket] - group * z.bins)
        partner = jnp.where(leaves, lax.div(source[bucket], jnp.int32(z.bins)), partner)
        end = jnp.int32(0)
        for k in range(z.slots):
            end = end + lengths[k, bucket]
            meta[z.ends + place * z.slots + k] = end
        kept_before = kept_before + (1 - leaving[m])
        left_before = left_before + leaving[m]
    receives = left_total > 0
    apart = group ^ partner
    top = jnp.int32(1)
    for k in range(1, z.groups):
        top = jnp.where(apart == k, 1 << (k.bit_length() - 1), top)
    sender = jnp.where(receives, partner, group)
    down = ((sender & top) != 0).astype(jnp.int32)
    meta[CHOSEN] = 2 * jnp.maximum(apart - 1, 0) + down
    meta[RECEIVES] = receives.astype(jnp.int32)
    for i in range(3):
        meta[GROUP + i] = ids[i]
    for copy in copies:
        copy.wait()


def book(z, source_bin, lengths, tokens, flat_out):
    block = jax.ShapeDtypeStruct((z.rows, z.width), tokens.dtype)
    first = jax.ShapeDtypeStruct((z.depth // 2, z.width), flat_out.dtype)
    return pl.pallas_call(
        functools.partial(book_kernel, z),
        out_shape=[jax.ShapeDtypeStruct((z.length,), jnp.int32)] + [block] * z.moved + [first],
        in_specs=[SMEM, SMEM, ANY, ANY],
        out_specs=[SMEM] + [VMEM] * (z.moved + 1),
        scratch_shapes=[pltpu.SemaphoreType.DMA((z.moved + 1,))],
        compiler_params=pltpu.CompilerParams(vmem_limit_bytes=60 * MIB),
        cost_estimate=COST,
        name="book",
    )(source_bin, lengths.T, tokens, flat_out)


def norm_kernel(z, buckets, after, meta, tokens, *rest):
    kept = z.count - z.moved
    arrived = sum(m >= kept for m in buckets)
    incoming, rest = rest[:arrived], rest[arrived:]
    affine = rest[:2]
    normed, blocks, gain, bias, sems = rest[2 + after :]
    copies = [
        pltpu.make_async_copy(affine[0], gain, sems.at[0]),
        pltpu.make_async_copy(affine[1], bias, sems.at[1]),
    ]
    for copy in copies:
        copy.start()
    own, other = [], {}
    for i, m in enumerate(buckets):
        own.append(
            pltpu.make_async_copy(tokens.at[meta[z.own + m]], blocks.at[i], sems.at[2 + i])
        )
        if m < kept:
            own[-1].start()
        else:
            source = incoming[len(other)]
            other[i] = pltpu.make_async_copy(source, blocks.at[i], sems.at[2 + i])
    if other:

        @pl.when(meta[RECEIVES] == 1)
        def _():
            for copy in other.values():
                copy.start()

        @pl.when(meta[RECEIVES] != 1)
        def _():
            for i in other:
                own[i].start()

    for copy in copies:
        copy.wait()
    step = 16
    for i in range(len(buckets)):
        own[i].wait()
        for r in range(0, z.rows, step):
            widened = blocks[i, r : r + step, :].astype(jnp.float32)
            average = jnp.mean(widened, axis=-1, keepdims=True)
            centred = widened - average
            spread = jnp.mean(centred * centred, axis=-1, keepdims=True)
            scaled = centred * lax.rsqrt(spread + 1e-05) * gain[...] + bias[...]
            at = i * z.rows + r
            normed[at : at + step, :] = scaled.astype(normed.dtype)


def normalise(z, buckets, meta, tokens, incoming, gain, bias, after=()):
    count = len(buckets)
    return pl.pallas_call(
        functools.partial(norm_kernel, z, buckets, len(after)),
        out_shape=jax.ShapeDtypeStruct((count * z.rows, z.width), tokens.dtype),
        in_specs=[SMEM, ANY] + [ANY] * (len(incoming) + 2 + len(after)),
        out_specs=VMEM,
        scratch_shapes=[
            pltpu.VMEM((count, z.rows, z.width), tokens.dtype),
            pltpu.VMEM((1, z.width), jnp.float32),
            pltpu.VMEM((1, z.width), jnp.float32),
            pltpu.SemaphoreType.DMA((2 + count,)),
        ],
        compiler_params=pltpu.CompilerParams(vmem_limit_bytes=60 * MIB),
        cost_estimate=COST,
        name="normalise",
    )(meta, tokens, *incoming, gain, bias, *after)


def slot_rows(z, meta, shape, axis):
    index = lax.broadcasted_iota(jnp.int32, shape, axis)
    piece = lax.div(index, jnp.int32(z.rows))
    return (meta[RANK] ^ piece) * z.rows + (index - piece * z.rows)


def members(z, meta, m, rows):
    member = jnp.zeros(rows.shape, jnp.int32)
    for k in range(z.slots):
        member = member + (rows >= meta[z.ends + m * z.slots + k]).astype(jnp.int32)
    return member


def tables(z, meta, m, rows, member):
    start = jnp.zeros(rows.shape, jnp.int32)
    for k in range(1, z.slots):
        start = jnp.where(member == k, meta[z.ends + m * z.slots + k - 1], start)
    position = (rows - start).astype(jnp.float32)
    lane = lax.broadcasted_iota(jnp.int32, (1, z.size), 1)
    half = z.size // 2
    index = jnp.where(lane < half, lane, lane - half).astype(jnp.float32)
    frequency = jnp.exp(index * jnp.float32(-2.0 / z.size * 9.210340371976184))
    angle = position * frequency
    turned = jnp.sin(angle)
    return jnp.cos(angle), jnp.where(lane < half, -turned, turned)


def attend_kernel(z, buckets, steps, swaps, after, meta, *rest):
    n, count = z.tensors, len(buckets)
    pieces, rest = rest[:n], rest[n:]
    weight, bias = rest[:2]
    rest = rest[2 + after :]
    outputs, rest = rest[:n], rest[n:]
    rows, held, total, cosine, sine, shift, sems = rest
    full = n * z.rows
    chunk = z.width // steps
    columns = z.kinds * z.depth
    fetches = []
    for s in range(steps):
        at = slice(s * chunk, (s + 1) * chunk)
        now = [pltpu.make_async_copy(weight.at[at], held.at[at], sems.at[s, 0])]
        for i in range(n * count):
            m, j = i // n, i % n
            now.append(
                pltpu.make_async_copy(
                    pieces[j].at[m * z.rows : (m + 1) * z.rows, at],
                    rows.at[i * z.rows : (i + 1) * z.rows, at],
                    sems.at[s, i + 1],
                )
            )
        if s == 0:
            now.append(pltpu.make_async_copy(bias, shift, sems.at[steps, 0]))
        for copy in now:
            copy.start()
        fetches.append(now)
    for i, m in enumerate(buckets):
        index = slot_rows(z, meta, (full, 1), 0)
        cosine[i], sine[i] = tables(z, meta, m, index, members(z, meta, m, index))
    for s in range(steps):
        at = slice(s * chunk, (s + 1) * chunk)
        for copy in fetches[s]:
            copy.wait()
        product = jnp.dot(rows[:, at], held[at, :], preferred_element_type=jnp.float32)
        if s == 0:
            total[...] = product + shift[...]
        else:
            total[...] += product
    for i, m in enumerate(buckets):
        row_member = members(z, meta, m, slot_rows(z, meta, (full, 1), 0))
        column_member = members(z, meta, m, slot_rows(z, meta, (1, full), 1))
        allowed = (row_member == column_member) & (column_member < z.slots)
        cos, sin = cosine[i], sine[i]

        def turn(u):
            return (u * cos + pltpu.roll(u, z.size // 2, 1) * sin).astype(jnp.bfloat16)

        def part(kind, h):
            place = (kind * z.heads + h) * z.size
            return total[i * full : (i + 1) * full, place : place + z.size]

        contexts = []
        for h in range(z.heads):
            queries = turn(part(0, h) * jnp.float32(z.size ** (-0.5)))
            key_rows = turn(part(1, h))
            values = part(2, h).astype(jnp.bfloat16)
            scores = lax.dot_general(
                queries, key_rows, (((1,), (1,)), ((), ())), preferred_element_type=jnp.float32
            )
            masked = jnp.where(allowed, scores, jnp.float32(-1e30))
            raised = jnp.exp(masked - jnp.max(masked, axis=-1, keepdims=True))
            share = raised / jnp.sum(raised, axis=-1, keepdims=True)
            contexts.append(
                jnp.dot(share.astype(jnp.bfloat16), values, preferred_element_type=jnp.float32)
            )
        plain = jnp.concatenate(contexts, axis=-1)
        half = z.depth // 2
        turned = plain
        if swaps:
            turned = jnp.concatenate([plain[:, half:], plain[:, :half]], axis=-1)
            turned = jnp.where(meta[PART] == 1, turned, plain)
        for j in range(n):
            value = (turned if j > 1 else plain)[j * z.rows : (j + 1) * z.rows]
            outputs[j][i * z.rows : (i + 1) * z.rows, :] = value.astype(jnp.bfloat16)


def attend(z, buckets, meta, pieces, weight, bias, swaps, after=()):
    steps = 5
    count = len(buckets)
    columns = z.kinds * z.depth
    full = z.rows * z.tensors
    return pl.pallas_call(
        functools.partial(attend_kernel, z, buckets, steps, swaps, len(after)),
        out_shape=[jax.ShapeDtypeStruct((count * z.rows, z.depth), jnp.bfloat16)] * z.tensors,
        in_specs=[SMEM] + [ANY] * (z.tensors + 2 + len(after)),
        out_specs=[VMEM] * z.tensors,
        scratch_shapes=[
            pltpu.VMEM((count * full, z.width), jnp.bfloat16),
            pltpu.VMEM((z.width, columns), jnp.bfloat16),
            pltpu.VMEM((count * full, columns), jnp.float32),
            pltpu.VMEM((count, full, z.size), jnp.float32),
            pltpu.VMEM((count, full, z.size), jnp.float32),
            pltpu.VMEM((1, columns), jnp.float32),
            pltpu.SemaphoreType.DMA((steps + 1, count * z.tensors + 1)),
        ],
        compiler_params=pltpu.CompilerParams(vmem_limit_bytes=60 * MIB),
        cost_estimate=pl.CostEstimate(
            flops=2 * count * full * z.width * columns,
            bytes_accessed=2 * z.width * (count * full + columns),
            transcendentals=count * z.heads * full * full,
        ),
        name="attend",
    )(meta, *pieces, weight, bias, *after)


def output_kernel(z, depths, counts, steps, meta, *rest):
    contexts, rest = rest[: len(counts) * z.tensors], rest[len(counts) * z.tensors :]
    weights, rest = rest[: len(depths)], rest[len(depths) :]
    tokens, incoming, bias, out = rest[0], rest[1 : 1 + z.moved], rest[1 + z.moved], rest[2 + z.moved]
    held, blocks, joined, ready, shift, sems, block_sems, out_sems, context_sems = rest[3 + z.moved :]
    chunk = z.width // steps
    small = [pltpu.make_async_copy(bias, shift, context_sems.at[0])]
    m = 0
    for g, count in enumerate(counts):
        for j in range(z.tensors):
            small.append(
                pltpu.make_async_copy(
                    contexts[g * z.tensors + j],
                    joined.at[m * z.rows : (m + count) * z.rows, j * z.depth : (j + 1) * z.depth],
                    context_sems.at[len(small)],
                )
            )
        m += count
    for copy in small:
        copy.start()
    fetches = []
    for s in range(steps):
        at = slice(s * chunk, (s + 1) * chunk)
        now = []
        place = 0
        for i, depth in enumerate(depths):
            now.append(
                pltpu.make_async_copy(
                    weights[i].at[:, at], held.at[place : place + depth, at], sems.at[s, i]
                )
            )
            now[-1].start()
            place += depth
        fetches.append(now)
        if s == 0:
            own = [
                pltpu.make_async_copy(
                    tokens.at[meta[z.own + m]], blocks.at[m], block_sems.at[m]
                )
                for m in range(z.count)
            ]
            kept = z.count - z.moved
            other = [
                pltpu.make_async_copy(incoming[k], blocks.at[kept + k], block_sems.at[kept + k])
                for k in range(z.moved)
            ]
            for m in range(kept):
                own[m].start()

            @pl.when(meta[RECEIVES] == 1)
            def _():
                for copy in other:
                    copy.start()

            @pl.when(meta[RECEIVES] != 1)
            def _():
                for copy in own[kept:]:
                    copy.start()

    for copy in small:
        copy.wait()
    index = meta[RANK] * z.rows + lax.broadcasted_iota(jnp.int32, (z.rows, 1), 0)
    leaving = []
    for s in range(steps):
        at = slice(s * chunk, (s + 1) * chunk)
        for copy in fetches[s]:
            copy.wait()
        total = jnp.dot(joined[...], held[:, at], preferred_element_type=jnp.float32)
        if s == 0:
            for copy in own:
                copy.wait()
        for m in range(z.count):
            block = blocks[m, :, at].astype(jnp.float32)
            value = block + total[m * z.rows : (m + 1) * z.rows] + shift[:, at]
            there = index < meta[z.ends + m * z.slots + z.slots - 1]
            ready[m, :, at] = jnp.where(there, value, jnp.float32(0.0)).astype(out.dtype)
            copy = pltpu.make_async_copy(
                ready.at[m, :, at], out.at[meta[z.order + m], :, at], out_sems.at[s, m]
            )
            copy.start()
            leaving.append(copy)
    for copy in leaving:
        copy.wait()


def project(z, meta, contexts, counts, weights, tokens, incoming, bias):
    steps = 5
    depths = [w.shape[0] for w in weights]
    flat = [c for bucket in contexts for c in bucket]
    return pl.pallas_call(
        functools.partial(output_kernel, z, depths, counts, steps),
        out_shape=jax.ShapeDtypeStruct((z.count, z.rows, z.width), tokens.dtype),
        in_specs=[SMEM] + [ANY] * (len(flat) + len(depths) + z.moved + 2),
        out_specs=ANY,
        scratch_shapes=[
            pltpu.VMEM((sum(depths), z.width), jnp.bfloat16),
            pltpu.VMEM((z.count, z.rows, z.width), tokens.dtype),
            pltpu.VMEM((z.count * z.rows, z.tensors * z.depth), jnp.bfloat16),
            pltpu.VMEM((z.count, z.rows, z.width), tokens.dtype),
            pltpu.VMEM((1, z.width), jnp.float32),
            pltpu.SemaphoreType.DMA((steps, len(depths))),
            pltpu.SemaphoreType.DMA((z.count,)),
            pltpu.SemaphoreType.DMA((steps, z.count)),
            pltpu.SemaphoreType.DMA((len(flat) + 1,)),
        ],
        compiler_params=pltpu.CompilerParams(vmem_limit_bytes=60 * MIB),
        cost_estimate=COST,
        name="project",
    )(meta, *flat, *weights, tokens, *incoming, bias)


def on_device(
    tokens, norm_gain, norm_bias, qkv_weight, qkv_bias, out_weight, out_bias, lengths, source_bin
):
    groups = lax.axis_size("dp")
    tensors = lax.axis_size("tensor")
    z = Sizes(tokens, lengths, qkv_weight, groups, tensors)
    flat_out = out_weight.reshape(z.depth, z.width)
    meta, *outgoing, half_out = book(z, source_bin, lengths, tokens, flat_out)

    gain, bias = norm_gain.reshape(1, -1), norm_bias.reshape(1, -1)
    qkv_row = jnp.transpose(qkv_bias, (1, 0, 2)).reshape(1, -1)
    split = lax.axis_size("parts") == 2 and tensors > 2
    kept = z.count - z.moved
    small = tensors <= 4

    def send_back(contexts):
        return [contexts[0]] + [exchange(contexts[j], "tensor", j) for j in range(1, tensors)]

    def relayout(weight):
        flat = jnp.transpose(weight, (0, 2, 1, 3)).reshape(z.width, z.kinds * z.depth)
        return with_layout_constraint(flat, Layout((0, 1)))

    def out_firsts():
        firsts = {0: half_out if split else flat_out}
        for mask in masks_of(tensors)[:-1]:
            for j in list(firsts):
                firsts[j | mask] = exchange(firsts[j], "tensor", mask)
        del firsts[0]
        return firsts

    def across(firsts):
        return {j: exchange(h, "parts", 1) for j, h in firsts.items()} if split else {}

    def work(buckets, pieces, weight):
        return attend(z, buckets, meta, pieces, weight, qkv_row, split)

    def start(buckets, incoming, after=()):
        sources = [incoming[m - kept] for m in buckets if m >= kept]
        return normalise(z, buckets, meta, tokens, sources, gain, bias, after)

    ways = []
    for k in range(1, groups):
        top = 1 << (k.bit_length() - 1)
        up = [(i, i ^ k) for i in range(groups) if not i & top]
        ways += [up, [(d, s) for s, d in up]]

    def choose(branch):
        return lax.switch(meta[CHOSEN], [functools.partial(branch, pairs) for pairs in ways])

    last = z.count - 1
    if small:

        first = list(range(last))

        def early(pairs):
            arrived = [lax.ppermute(block, "dp", pairs) for block in outgoing[:-1]]
            return arrived, out_firsts(), relayout(qkv_weight)

        arrived, firsts, weight = choose(early)
        seconds = across(firsts)

        def late(pairs):
            arriving = lax.ppermute(outgoing[-1], "dp", pairs)
            own = start(first, arrived)
            return arriving, own, hop(own)

        arriving, own, crossed = choose(late)
        held = gather_xor(own, crossed)
        incoming = arrived + [arriving]
        normed = start([last], incoming, list(seconds.values()))
        counts = [last, 1]
        contexts = [send_back(work(first, held, weight))]
        pieces = gather_xor(normed, None, contexts[0][0])
        contexts.append(send_back(work([last], pieces, weight)))
    else:
        incoming = choose(lambda pairs: [lax.ppermute(b, "dp", pairs) for b in outgoing])
        weight = relayout(qkv_weight)
        firsts = out_firsts()
        seconds = across(firsts)
        counts = [1] * z.count
        contexts = [
            send_back(work([m], gather_xor(start([m], incoming)), weight))
            for m in range(z.count)
        ]

    rows_of = {0: [flat_out]}
    if tensors > 1:
        rows_of[1] = [exchange(flat_out, "tensor", 1)]
    for j in firsts:
        held = [firsts[j]]
        rows_of[j | 1] = [exchange(firsts[j], "tensor", 1)]
        if split:
            second = seconds[j]
            held.append(second)
            second, _ = lax.optimization_barrier((second, contexts[-1][0]))
            rows_of[j | 1].append(exchange(second, "tensor", 1))
        rows_of[j] = held
    weights = [h for j in range(tensors) for h in rows_of[j]]
    return project(z, meta, contexts, counts, weights, tokens, incoming, out_bias.reshape(1, -1))


def solution(mesh):
    return jax.shard_map(
        on_device,
        mesh=mesh,
        in_specs=(
            P(("parts", "dp"), "tensor", None),
            P(),
            P(),
            P(None, "tensor", None, None),
            P("tensor", None, None),
            P("tensor", None, None),
            P(),
            P("parts", None),
            P("parts"),
        ),
        out_specs=P(("parts", "dp"), "tensor", None),
        check_vma=False,
    )
```

```python
import functools

import jax
import jax.numpy as jnp
from jax import lax
from jax.experimental import pallas as pl
from jax.experimental.layout import Layout, with_layout_constraint
from jax.experimental.pallas import tpu as pltpu
from jax.sharding import PartitionSpec as P

MIB = 1 << 20
COST = pl.CostEstimate(flops=0, bytes_accessed=0, transcendentals=0)
CHOSEN, RECEIVES, GROUP, RANK, PART, FIRST = 0, 1, 2, 3, 4, 8
ANY = pl.BlockSpec(memory_space=pl.ANY)
SMEM = pl.BlockSpec(memory_space=pltpu.SMEM)
VMEM = pl.BlockSpec(memory_space=pltpu.VMEM)


def exchange(value, axis, mask):
    size = lax.axis_size(axis)
    return lax.ppermute(value, axis, [(i, i ^ mask) for i in range(size)])


def masks_of(size):
    mask = size // 2
    result = []
    while mask:
        result.append(mask)
        mask //= 2
    return result


def hop(own):
    return exchange(own, "tensor", lax.axis_size("tensor") // 2)


def gather_xor(own, crossed=None, after=None):
    pieces = {0: own}
    for mask in masks_of(lax.axis_size("tensor")):
        for j in list(pieces):
            piece = pieces[j]
            if crossed is not None and len(pieces) == 1:
                pieces[j | mask] = crossed
                continue
            if j and after is not None:
                piece, _ = lax.optimization_barrier((piece, after))
            pieces[j | mask] = exchange(piece, "tensor", mask)
    return [pieces[j] for j in range(len(pieces))]


class Sizes:
    def __init__(self, tokens, lengths, qkv_weight, groups, tensors):
        self.bins, self.rows, self.width = tokens.shape
        self.slots = lengths.shape[-1]
        self.buckets = lengths.shape[0]
        self.groups = groups
        self.tensors = tensors
        self.count = self.buckets // groups
        self.moved = self.bins - self.count
        self.heads, self.kinds, self.size = qkv_weight.shape[1:]
        self.depth = self.heads * self.size
        self.order = FIRST
        self.own = self.order + self.count
        self.sent = self.own + self.count
        self.ends = self.sent + self.moved + 1
        self.length = self.ends + self.count * self.slots


def book_kernel(z, source, lengths, tokens, out_weight, meta, *rest):
    outgoing, first, sems = rest[:-2], rest[-2], rest[-1]
    ids = [lax.axis_index(axis) for axis in ("dp", "tensor", "parts")]
    group = ids[0]
    deep = first.shape[0]
    copies = [
        pltpu.make_async_copy(
            out_weight.at[pl.ds(pl.multiple_of(ids[2] * deep, deep), deep)],
            first,
            sems.at[z.moved],
        )
    ]
    copies[0].start()
    for i in range(z.length):
        meta[i] = jnp.int32(0)
    sent = jnp.int32(0)
    partner = jnp.int32(0)
    for b in range(z.buckets):
        owner = b // z.count
        place = source[b] - group * z.bins
        here = (place >= 0) & (place < z.bins) & (owner != group)
        meta[z.sent + jnp.where(here, jnp.minimum(sent, z.moved), z.moved)] = jnp.where(
            here, place, 0
        )
        sent = sent + here.astype(jnp.int32)
        partner = jnp.where(here, owner, partner)
    for m in range(z.moved):
        copies.append(
            pltpu.make_async_copy(tokens.at[meta[z.sent + m]], outgoing[m], sems.at[m])
        )
        copies[-1].start()
    leaving = []
    for m in range(z.count):
        place = source[group * z.count + m] - group * z.bins
        leaving.append(((place < 0) | (place >= z.bins)).astype(jnp.int32))
    left_total = functools.reduce(lambda a, b: a + b, leaving)
    kept_before = jnp.int32(0)
    left_before = z.count - left_total
    for m in range(z.count):
        bucket = group * z.count + m
        leaves = leaving[m] == 1
        place = jnp.where(leaves, left_before, kept_before)
        meta[z.order + place] = jnp.int32(m)
        meta[z.own + place] = jnp.where(leaves, 0, source[bucket] - group * z.bins)
        partner = jnp.where(leaves, lax.div(source[bucket], jnp.int32(z.bins)), partner)
        end = jnp.int32(0)
        for k in range(z.slots):
            end = end + lengths[k, bucket]
            meta[z.ends + place * z.slots + k] = end
        kept_before = kept_before + (1 - leaving[m])
        left_before = left_before + leaving[m]
    receives = left_total > 0
    apart = group ^ partner
    top = jnp.int32(1)
    for k in range(1, z.groups):
        top = jnp.where(apart == k, 1 << (k.bit_length() - 1), top)
    sender = jnp.where(receives, partner, group)
    down = ((sender & top) != 0).astype(jnp.int32)
    meta[CHOSEN] = 2 * jnp.maximum(apart - 1, 0) + down
    meta[RECEIVES] = receives.astype(jnp.int32)
    for i in range(3):
        meta[GROUP + i] = ids[i]
    for copy in copies:
        copy.wait()


def book(z, source_bin, lengths, tokens, flat_out):
    block = jax.ShapeDtypeStruct((z.rows, z.width), tokens.dtype)
    first = jax.ShapeDtypeStruct((z.depth // 2, z.width), flat_out.dtype)
    return pl.pallas_call(
        functools.partial(book_kernel, z),
        out_shape=[jax.ShapeDtypeStruct((z.length,), jnp.int32)] + [block] * z.moved + [first],
        in_specs=[SMEM, SMEM, ANY, ANY],
        out_specs=[SMEM] + [VMEM] * (z.moved + 1),
        scratch_shapes=[pltpu.SemaphoreType.DMA((z.moved + 1,))],
        compiler_params=pltpu.CompilerParams(vmem_limit_bytes=60 * MIB),
        cost_estimate=COST,
        name="book",
    )(source_bin, lengths.T, tokens, flat_out)


def norm_kernel(z, buckets, after, meta, tokens, *rest):
    kept = z.count - z.moved
    arrived = sum(m >= kept for m in buckets)
    incoming, rest = rest[:arrived], rest[arrived:]
    affine = rest[:2]
    normed, blocks, gain, bias, sems = rest[2 + after :]
    copies = [
        pltpu.make_async_copy(affine[0], gain, sems.at[0]),
        pltpu.make_async_copy(affine[1], bias, sems.at[1]),
    ]
    for copy in copies:
        copy.start()
    own, other = [], {}
    for i, m in enumerate(buckets):
        own.append(
            pltpu.make_async_copy(tokens.at[meta[z.own + m]], blocks.at[i], sems.at[2 + i])
        )
        if m < kept:
            own[-1].start()
        else:
            source = incoming[len(other)]
            other[i] = pltpu.make_async_copy(source, blocks.at[i], sems.at[2 + i])
    if other:

        @pl.when(meta[RECEIVES] == 1)
        def _():
            for copy in other.values():
                copy.start()

        @pl.when(meta[RECEIVES] != 1)
        def _():
            for i in other:
                own[i].start()

    for copy in copies:
        copy.wait()
    step = 16
    for i in range(len(buckets)):
        own[i].wait()
        for r in range(0, z.rows, step):
            widened = blocks[i, r : r + step, :].astype(jnp.float32)
            average = jnp.mean(widened, axis=-1, keepdims=True)
            centred = widened - average
            spread = jnp.mean(centred * centred, axis=-1, keepdims=True)
            scaled = centred * lax.rsqrt(spread + 1e-05) * gain[...] + bias[...]
            at = i * z.rows + r
            normed[at : at + step, :] = scaled.astype(normed.dtype)


def normalise(z, buckets, meta, tokens, incoming, gain, bias, after=()):
    count = len(buckets)
    return pl.pallas_call(
        functools.partial(norm_kernel, z, buckets, len(after)),
        out_shape=jax.ShapeDtypeStruct((count * z.rows, z.width), tokens.dtype),
        in_specs=[SMEM, ANY] + [ANY] * (len(incoming) + 2 + len(after)),
        out_specs=VMEM,
        scratch_shapes=[
            pltpu.VMEM((count, z.rows, z.width), tokens.dtype),
            pltpu.VMEM((1, z.width), jnp.float32),
            pltpu.VMEM((1, z.width), jnp.float32),
            pltpu.SemaphoreType.DMA((2 + count,)),
        ],
        compiler_params=pltpu.CompilerParams(vmem_limit_bytes=24 * MIB),
        cost_estimate=COST,
        name="normalise",
    )(meta, tokens, *incoming, gain, bias, *after)


def slot_rows(z, meta, shape, axis):
    index = lax.broadcasted_iota(jnp.int32, shape, axis)
    piece = lax.div(index, jnp.int32(z.rows))
    return (meta[RANK] ^ piece) * z.rows + (index - piece * z.rows)


def members(z, meta, m, rows):
    member = jnp.zeros(rows.shape, jnp.int32)
    for k in range(z.slots):
        member = member + (rows >= meta[z.ends + m * z.slots + k]).astype(jnp.int32)
    return member


def positions(z, meta, m):
    rows = slot_rows(z, meta, (z.rows * z.tensors, 1), 0)
    member = members(z, meta, m, rows)
    start = jnp.zeros(rows.shape, jnp.int32)
    for k in range(1, z.slots):
        start = jnp.where(member == k, meta[z.ends + m * z.slots + k - 1], start)
    return (rows - start).astype(jnp.float32)


def tables(z, meta, m, cosine, sine):
    position = positions(z, meta, m)
    split, half = z.rows * z.tensors // 2, z.size // 2
    lane = lax.broadcasted_iota(jnp.int32, (1, z.size), 1)
    front = lane < half
    index = jnp.where(front, lane, lane - half).astype(jnp.float32)
    frequency = jnp.exp(index * jnp.float32(-2.0 / z.size * 9.210340371976184))
    angle = jnp.where(front, position[:split], position[split:]) * frequency
    c, t = jnp.cos(angle), jnp.sin(angle)
    other_c, other_t = pltpu.roll(c, half, 1), pltpu.roll(t, half, 1)
    cosine[:split, :] = jnp.where(front, c, other_c)
    cosine[split:, :] = jnp.where(front, other_c, c)
    sine[:split, :] = jnp.where(front, -t, other_t)
    sine[split:, :] = jnp.where(front, -other_t, t)


def attend_kernel(z, buckets, later, ready, steps, swaps, book, *rest):
    n, count = z.tensors, len(buckets)
    pieces, rest = rest[:n], rest[n:]
    weight, bias, rest = rest[0], rest[1], rest[2:]
    given, rest = rest[: 2 * ready], rest[2 * ready :]
    earlier, rest = rest[: n * ready], rest[n * ready :]
    before = earlier[0].shape[0] if ready else 0
    outputs, rest = rest[:n], rest[n:]
    made, rest = rest[: 2 * len(later)], rest[2 * len(later) :]
    rows, held, total, cosine, sine, shift, meta, sems, meta_sem = rest
    kept = pltpu.make_async_copy(book, meta, meta_sem)
    full = n * z.rows
    chunk = z.width // steps
    fetches = []
    for s in range(steps):
        at = slice(s * chunk, (s + 1) * chunk)
        now = []
        now.append(pltpu.make_async_copy(weight.at[at], held.at[at], sems.at[s, 0]))
        for i in range(n * count):
            m, j = i // n, i % n
            now.append(
                pltpu.make_async_copy(
                    pieces[j].at[m * z.rows : (m + 1) * z.rows, at],
                    rows.at[i * z.rows : (i + 1) * z.rows, at],
                    sems.at[s, i + 1],
                )
            )
        if s == 0:
            now.append(pltpu.make_async_copy(bias, shift, sems.at[steps, 0]))
        if s == steps - 1 and ready:
            now.append(pltpu.make_async_copy(given[0], cosine.at[0], sems.at[steps, 1]))
            now.append(pltpu.make_async_copy(given[1], sine.at[0], sems.at[steps, 2]))
            for j in range(n):
                now.append(
                    pltpu.make_async_copy(
                        earlier[j], outputs[j].at[0:before], sems.at[steps, 3 + j]
                    )
                )
        for copy in now:
            copy.start()
        if s == 0:
            kept.start()
        fetches.append(now)
    kept.wait()
    if not ready:
        for i, m in enumerate(buckets):
            tables(z, meta, m, cosine.at[i], sine.at[i])
    for i, m in enumerate(later):
        tables(z, meta, m, made[2 * i], made[2 * i + 1])
    for s in range(steps):
        at = slice(s * chunk, (s + 1) * chunk)
        for copy in fetches[s]:
            copy.wait()
        product = jnp.dot(rows[:, at], held[at, :], preferred_element_type=jnp.float32)
        if s == 0:
            total[...] = product + shift[...]
        else:
            total[...] += product
    for i, m in enumerate(buckets):
        row_member = members(z, meta, m, slot_rows(z, meta, (full, 1), 0))
        column_member = members(z, meta, m, slot_rows(z, meta, (1, full), 1))
        allowed = (row_member == column_member) & (column_member < z.slots)
        cos, sin = cosine[i], sine[i]

        def turn(u):
            return (u * cos + pltpu.roll(u, z.size // 2, 1) * sin).astype(jnp.bfloat16)

        def part(kind, h):
            place = (kind * z.heads + h) * z.size
            return total[i * full : (i + 1) * full, place : place + z.size]

        contexts = []
        for h in range(z.heads):
            queries = turn(part(0, h) * jnp.float32(z.size ** (-0.5)))
            key_rows = turn(part(1, h))
            values = part(2, h).astype(jnp.bfloat16)
            scores = lax.dot_general(
                queries, key_rows, (((1,), (1,)), ((), ())), preferred_element_type=jnp.float32
            )
            masked = jnp.where(allowed, scores, jnp.float32(-1e30))
            raised = jnp.exp(masked - jnp.max(masked, axis=-1, keepdims=True))
            share = raised / jnp.sum(raised, axis=-1, keepdims=True)
            contexts.append(
                jnp.dot(share.astype(jnp.bfloat16), values, preferred_element_type=jnp.float32)
            )
        plain = jnp.concatenate(contexts, axis=-1)
        half = z.depth // 2
        turned = plain
        if swaps:
            turned = jnp.concatenate([plain[:, half:], plain[:, :half]], axis=-1)
            turned = jnp.where(meta[PART] == 1, turned, plain)
        for j in range(n):
            value = (turned if j > 1 else plain)[j * z.rows : (j + 1) * z.rows]
            at = before + i * z.rows
            outputs[j][at : at + z.rows, :] = value.astype(jnp.bfloat16)


def attend(z, buckets, later, meta, pieces, weight, bias, given, swaps):
    steps = 5
    count = len(buckets)
    before = given[2].shape[0] if given else 0
    columns = z.kinds * z.depth
    full = z.rows * z.tensors
    table = jax.ShapeDtypeStruct((full, z.size), jnp.float32)
    result = pl.pallas_call(
        functools.partial(attend_kernel, z, buckets, later, bool(given), steps, swaps),
        out_shape=[jax.ShapeDtypeStruct((before + count * z.rows, z.depth), jnp.bfloat16)] * z.tensors
        + [table] * (2 * len(later)),
        in_specs=[ANY] * (z.tensors + 3 + len(given)),
        out_specs=[VMEM] * (z.tensors + 2 * len(later)),
        scratch_shapes=[
            pltpu.VMEM((count * full, z.width), jnp.bfloat16),
            pltpu.VMEM((z.width, columns), jnp.bfloat16),
            pltpu.VMEM((count * full, columns), jnp.float32),
            pltpu.VMEM((count, full, z.size), jnp.float32),
            pltpu.VMEM((count, full, z.size), jnp.float32),
            pltpu.VMEM((1, columns), jnp.float32),
            pltpu.SMEM((z.length,), jnp.int32),
            pltpu.SemaphoreType.DMA((steps + 1, count * z.tensors + 3)),
            pltpu.SemaphoreType.DMA,
        ],
        compiler_params=pltpu.CompilerParams(vmem_limit_bytes=24 * MIB),
        cost_estimate=pl.CostEstimate(
            flops=2 * count * full * z.width * columns,
            bytes_accessed=2 * z.width * (count * full + columns),
            transcendentals=count * z.heads * full * full,
        ),
        name="attend",
    )(meta, *pieces, weight, bias, *given)
    return result[: z.tensors], result[z.tensors :]


def output_kernel(z, depths, counts, steps, meta, *rest):
    contexts, rest = rest[: len(counts) * z.tensors], rest[len(counts) * z.tensors :]
    weights, rest = rest[: len(depths)], rest[len(depths) :]
    tokens, incoming, bias, out = rest[0], rest[1 : 1 + z.moved], rest[1 + z.moved], rest[2 + z.moved]
    held, blocks, joined, ready, shift, sems, block_sems, out_sems, context_sems = rest[3 + z.moved :]
    chunk = z.width // steps
    small = [pltpu.make_async_copy(bias, shift, context_sems.at[0])]
    m = 0
    for g, count in enumerate(counts):
        for j in range(z.tensors):
            small.append(
                pltpu.make_async_copy(
                    contexts[g * z.tensors + j],
                    joined.at[m * z.rows : (m + count) * z.rows, j * z.depth : (j + 1) * z.depth],
                    context_sems.at[len(small)],
                )
            )
        m += count
    for copy in small:
        copy.start()
    fetches = []
    for s in range(steps):
        at = slice(s * chunk, (s + 1) * chunk)
        now = []
        place = 0
        for i, depth in enumerate(depths):
            now.append(
                pltpu.make_async_copy(
                    weights[i].at[:, at], held.at[place : place + depth, at], sems.at[s, i]
                )
            )
            now[-1].start()
            place += depth
        fetches.append(now)
        if s == 0:
            own = [
                pltpu.make_async_copy(
                    tokens.at[meta[z.own + m]], blocks.at[m], block_sems.at[m]
                )
                for m in range(z.count)
            ]
            kept = z.count - z.moved
            other = [
                pltpu.make_async_copy(incoming[k], blocks.at[kept + k], block_sems.at[kept + k])
                for k in range(z.moved)
            ]
            for m in range(kept):
                own[m].start()

            @pl.when(meta[RECEIVES] == 1)
            def _():
                for copy in other:
                    copy.start()

            @pl.when(meta[RECEIVES] != 1)
            def _():
                for copy in own[kept:]:
                    copy.start()

    for copy in small:
        copy.wait()
    index = meta[RANK] * z.rows + lax.broadcasted_iota(jnp.int32, (z.rows, 1), 0)
    leaving = []
    for s in range(steps):
        at = slice(s * chunk, (s + 1) * chunk)
        for copy in fetches[s]:
            copy.wait()
        total = jnp.dot(joined[...], held[:, at], preferred_element_type=jnp.float32)
        if s == 0:
            for copy in own:
                copy.wait()
        for m in range(z.count):
            block = blocks[m, :, at].astype(jnp.float32)
            value = block + total[m * z.rows : (m + 1) * z.rows] + shift[:, at]
            there = index < meta[z.ends + m * z.slots + z.slots - 1]
            ready[m, :, at] = jnp.where(there, value, jnp.float32(0.0)).astype(out.dtype)
            copy = pltpu.make_async_copy(
                ready.at[m, :, at], out.at[meta[z.order + m], :, at], out_sems.at[s, m]
            )
            copy.start()
            leaving.append(copy)
    for copy in leaving:
        copy.wait()


def project(z, meta, contexts, counts, weights, tokens, incoming, bias):
    steps = 5
    depths = [w.shape[0] for w in weights]
    flat = [c for bucket in contexts for c in bucket]
    return pl.pallas_call(
        functools.partial(output_kernel, z, depths, counts, steps),
        out_shape=jax.ShapeDtypeStruct((z.count, z.rows, z.width), tokens.dtype),
        in_specs=[SMEM] + [ANY] * (len(flat) + len(depths) + z.moved + 2),
        out_specs=ANY,
        scratch_shapes=[
            pltpu.VMEM((sum(depths), z.width), jnp.bfloat16),
            pltpu.VMEM((z.count, z.rows, z.width), tokens.dtype),
            pltpu.VMEM((z.count * z.rows, z.tensors * z.depth), jnp.bfloat16),
            pltpu.VMEM((z.count, z.rows, z.width), tokens.dtype),
            pltpu.VMEM((1, z.width), jnp.float32),
            pltpu.SemaphoreType.DMA((steps, len(depths))),
            pltpu.SemaphoreType.DMA((z.count,)),
            pltpu.SemaphoreType.DMA((steps, z.count)),
            pltpu.SemaphoreType.DMA((len(flat) + 1,)),
        ],
        compiler_params=pltpu.CompilerParams(vmem_limit_bytes=14 * MIB + 2 * sum(depths) * z.width),
        cost_estimate=COST,
        name="project",
    )(meta, *flat, *weights, tokens, *incoming, bias)


def on_device(
    tokens, norm_gain, norm_bias, qkv_weight, qkv_bias, out_weight, out_bias, lengths, source_bin
):
    groups = lax.axis_size("dp")
    tensors = lax.axis_size("tensor")
    z = Sizes(tokens, lengths, qkv_weight, groups, tensors)
    flat_out = out_weight.reshape(z.depth, z.width)
    meta, *outgoing, half_out = book(z, source_bin, lengths, tokens, flat_out)

    gain, bias = norm_gain.reshape(1, -1), norm_bias.reshape(1, -1)
    qkv_row = jnp.transpose(qkv_bias, (1, 0, 2)).reshape(1, -1)
    split = lax.axis_size("parts") == 2 and tensors > 2
    kept = z.count - z.moved
    small = tensors <= 4

    def send_back(contexts):
        return [contexts[0]] + [exchange(contexts[j], "tensor", j) for j in range(1, tensors)]

    def relayout(weight):
        flat = jnp.transpose(weight, (0, 2, 1, 3)).reshape(z.width, z.kinds * z.depth)
        return with_layout_constraint(flat, Layout((0, 1)))

    def out_firsts():
        firsts = {0: half_out if split else flat_out}
        for mask in masks_of(tensors)[:-1]:
            for j in list(firsts):
                firsts[j | mask] = exchange(firsts[j], "tensor", mask)
        del firsts[0]
        return firsts

    def across(firsts):
        return {j: exchange(h, "parts", 1) for j, h in firsts.items()} if split else {}

    def work(buckets, pieces, weight, later=(), given=()):
        return attend(z, buckets, later, meta, pieces, weight, qkv_row, given, split)

    def start(buckets, incoming, after=()):
        sources = [incoming[m - kept] for m in buckets if m >= kept]
        return normalise(z, buckets, meta, tokens, sources, gain, bias, after)

    ways = []
    for k in range(1, groups):
        top = 1 << (k.bit_length() - 1)
        up = [(i, i ^ k) for i in range(groups) if not i & top]
        ways += [up, [(d, s) for s, d in up]]

    def choose(branch):
        return lax.switch(meta[CHOSEN], [functools.partial(branch, pairs) for pairs in ways])

    last = z.count - 1
    if small:

        first = list(range(last))

        def early(pairs):
            arrived = [lax.ppermute(block, "dp", pairs) for block in outgoing[:-1]]
            weight = relayout(qkv_weight)
            return arrived, out_firsts(), weight, start(first, arrived, (weight,))

        arrived, firsts, weight, own = choose(early)
        seconds = across(firsts)

        def late(pairs):
            arriving = lax.ppermute(outgoing[-1], "dp", pairs)
            return arriving, hop(own)

        arriving, crossed = choose(late)
        held = gather_xor(own, crossed)
        incoming = arrived + [arriving]
        normed = start([last], incoming, list(seconds.values()))
        counts = [z.count]
        context, made = work(first, held, weight, [last])
        pieces = gather_xor(normed, None, context[0])
        context, _ = work([last], pieces, weight, (), [*made, *context])
        contexts = [send_back(context)]
    else:
        incoming = choose(lambda pairs: [lax.ppermute(b, "dp", pairs) for b in outgoing])
        weight = relayout(qkv_weight)
        firsts = out_firsts()
        seconds = across(firsts)
        counts = [1] * z.count
        contexts = [
            send_back(work([m], gather_xor(start([m], incoming)), weight)[0])
            for m in range(z.count)
        ]

    rows_of = {0: [flat_out]}
    if tensors > 1:
        rows_of[1] = [exchange(flat_out, "tensor", 1)]
    for j in firsts:
        held = [firsts[j]]
        rows_of[j | 1] = [exchange(firsts[j], "tensor", 1)]
        if split:
            second = seconds[j]
            held.append(second)
            second, _ = lax.optimization_barrier((second, contexts[-1][0]))
            rows_of[j | 1].append(exchange(second, "tensor", 1))
        rows_of[j] = held
    weights = [h for j in range(tensors) for h in rows_of[j]]
    return project(z, meta, contexts, counts, weights, tokens, incoming, out_bias.reshape(1, -1))


def solution(mesh):
    return jax.shard_map(
        on_device,
        mesh=mesh,
        in_specs=(
            P(("parts", "dp"), "tensor", None),
            P(),
            P(),
            P(None, "tensor", None, None),
            P("tensor", None, None),
            P("tensor", None, None),
            P(),
            P("parts", None),
            P("parts"),
        ),
        out_specs=P(("parts", "dp"), "tensor", None),
        check_vma=False,
    )
```

```python
import functools

import jax
import jax.numpy as jnp
from jax import lax
from jax.experimental import pallas as pl
from jax.experimental.layout import Layout, with_layout_constraint
from jax.experimental.pallas import tpu as pltpu
from jax.sharding import PartitionSpec as P

MIB = 1 << 20
COST = pl.CostEstimate(flops=0, bytes_accessed=0, transcendentals=0)
CHOSEN, RECEIVES, GROUP, RANK, PART, FIRST = 0, 1, 2, 3, 4, 8
ANY = pl.BlockSpec(memory_space=pl.ANY)
SMEM = pl.BlockSpec(memory_space=pltpu.SMEM)
VMEM = pl.BlockSpec(memory_space=pltpu.VMEM)


def exchange(value, axis, mask):
    size = lax.axis_size(axis)
    return lax.ppermute(value, axis, [(i, i ^ mask) for i in range(size)])


def masks_of(size):
    mask = size // 2
    result = []
    while mask:
        result.append(mask)
        mask //= 2
    return result


def hop(own):
    return exchange(own, "tensor", lax.axis_size("tensor") // 2)


def gather_xor(own, crossed=None, after=None, beside=None):
    pieces = {0: own}
    for mask in masks_of(lax.axis_size("tensor")):
        for j in list(pieces):
            piece = pieces[j]
            if crossed is not None and len(pieces) == 1:
                pieces[j | mask] = crossed
                continue
            if beside is not None and j | mask == 1:
                pieces[1] = beside
                continue
            if j and after is not None:
                piece, _ = lax.optimization_barrier((piece, after))
            pieces[j | mask] = exchange(piece, "tensor", mask)
    return [pieces[j] for j in range(len(pieces))]


class Sizes:
    def __init__(self, tokens, lengths, qkv_weight, groups, tensors):
        self.bins, self.rows, self.width = tokens.shape
        self.slots = lengths.shape[-1]
        self.buckets = lengths.shape[0]
        self.groups = groups
        self.tensors = tensors
        self.count = self.buckets // groups
        self.moved = self.bins - self.count
        self.heads, self.kinds, self.size = qkv_weight.shape[1:]
        self.depth = self.heads * self.size
        self.order = FIRST
        self.own = self.order + self.count
        self.sent = self.own + self.count
        self.ends = self.sent + self.moved + 1
        self.length = self.ends + self.count * self.slots


def book_kernel(z, source, lengths, tokens, out_weight, meta, *rest):
    outgoing, first, sems = rest[:-2], rest[-2], rest[-1]
    ids = [lax.axis_index(axis) for axis in ("dp", "tensor", "parts")]
    group = ids[0]
    deep = first.shape[0]
    copies = [
        pltpu.make_async_copy(
            out_weight.at[pl.ds(pl.multiple_of(ids[2] * deep, deep), deep)],
            first,
            sems.at[z.moved],
        )
    ]
    copies[0].start()
    for i in range(z.length):
        meta[i] = jnp.int32(0)
    sent = jnp.int32(0)
    partner = jnp.int32(0)
    for b in range(z.buckets):
        owner = b // z.count
        place = source[b] - group * z.bins
        here = (place >= 0) & (place < z.bins) & (owner != group)
        meta[z.sent + jnp.where(here, jnp.minimum(sent, z.moved), z.moved)] = jnp.where(
            here, place, 0
        )
        sent = sent + here.astype(jnp.int32)
        partner = jnp.where(here, owner, partner)
    for m in range(z.moved):
        copies.append(
            pltpu.make_async_copy(tokens.at[meta[z.sent + m]], outgoing[m], sems.at[m])
        )
        copies[-1].start()
    leaving = []
    for m in range(z.count):
        place = source[group * z.count + m] - group * z.bins
        leaving.append(((place < 0) | (place >= z.bins)).astype(jnp.int32))
    left_total = functools.reduce(lambda a, b: a + b, leaving)
    kept_before = jnp.int32(0)
    left_before = z.count - left_total
    for m in range(z.count):
        bucket = group * z.count + m
        leaves = leaving[m] == 1
        place = jnp.where(leaves, left_before, kept_before)
        meta[z.order + place] = jnp.int32(m)
        meta[z.own + place] = jnp.where(leaves, 0, source[bucket] - group * z.bins)
        partner = jnp.where(leaves, lax.div(source[bucket], jnp.int32(z.bins)), partner)
        end = jnp.int32(0)
        for k in range(z.slots):
            end = end + lengths[k, bucket]
            meta[z.ends + place * z.slots + k] = end
        kept_before = kept_before + (1 - leaving[m])
        left_before = left_before + leaving[m]
    receives = left_total > 0
    apart = group ^ partner
    top = jnp.int32(1)
    for k in range(1, z.groups):
        top = jnp.where(apart == k, 1 << (k.bit_length() - 1), top)
    sender = jnp.where(receives, partner, group)
    down = ((sender & top) != 0).astype(jnp.int32)
    meta[CHOSEN] = 2 * jnp.maximum(apart - 1, 0) + down
    meta[RECEIVES] = receives.astype(jnp.int32)
    for i in range(3):
        meta[GROUP + i] = ids[i]
    for copy in copies:
        copy.wait()


def book(z, source_bin, lengths, tokens, flat_out):
    block = jax.ShapeDtypeStruct((z.rows, z.width), tokens.dtype)
    first = jax.ShapeDtypeStruct((z.depth // 2, z.width), flat_out.dtype)
    return pl.pallas_call(
        functools.partial(book_kernel, z),
        out_shape=[jax.ShapeDtypeStruct((z.length,), jnp.int32)] + [block] * z.moved + [first],
        in_specs=[SMEM, SMEM, ANY, ANY],
        out_specs=[SMEM] + [VMEM] * (z.moved + 1),
        scratch_shapes=[pltpu.SemaphoreType.DMA((z.moved + 1,))],
        compiler_params=pltpu.CompilerParams(vmem_limit_bytes=60 * MIB),
        cost_estimate=COST,
        name="book",
    )(source_bin, lengths.T, tokens, flat_out)


def norm_kernel(z, buckets, after, meta, tokens, *rest):
    kept = z.count - z.moved
    arrived = sum(m >= kept for m in buckets)
    incoming, rest = rest[:arrived], rest[arrived:]
    affine = rest[:2]
    normed, blocks, gain, bias, sems = rest[2 + after :]
    copies = [
        pltpu.make_async_copy(affine[0], gain, sems.at[0]),
        pltpu.make_async_copy(affine[1], bias, sems.at[1]),
    ]
    for copy in copies:
        copy.start()
    own, other = [], {}
    for i, m in enumerate(buckets):
        own.append(
            pltpu.make_async_copy(tokens.at[meta[z.own + m]], blocks.at[i], sems.at[2 + i])
        )
        if m < kept:
            own[-1].start()
        else:
            source = incoming[len(other)]
            other[i] = pltpu.make_async_copy(source, blocks.at[i], sems.at[2 + i])
    if other:

        @pl.when(meta[RECEIVES] == 1)
        def _():
            for copy in other.values():
                copy.start()

        @pl.when(meta[RECEIVES] != 1)
        def _():
            for i in other:
                own[i].start()

    for copy in copies:
        copy.wait()
    step = 16
    for i in range(len(buckets)):
        own[i].wait()
        for r in range(0, z.rows, step):
            widened = blocks[i, r : r + step, :].astype(jnp.float32)
            average = jnp.mean(widened, axis=-1, keepdims=True)
            centred = widened - average
            spread = jnp.mean(centred * centred, axis=-1, keepdims=True)
            scaled = centred * lax.rsqrt(spread + 1e-05) * gain[...] + bias[...]
            at = i * z.rows + r
            normed[at : at + step, :] = scaled.astype(normed.dtype)


def normalise(z, buckets, meta, tokens, incoming, gain, bias, after=()):
    count = len(buckets)
    return pl.pallas_call(
        functools.partial(norm_kernel, z, buckets, len(after)),
        out_shape=jax.ShapeDtypeStruct((count * z.rows, z.width), tokens.dtype),
        in_specs=[SMEM, ANY] + [ANY] * (len(incoming) + 2 + len(after)),
        out_specs=VMEM,
        scratch_shapes=[
            pltpu.VMEM((count, z.rows, z.width), tokens.dtype),
            pltpu.VMEM((1, z.width), jnp.float32),
            pltpu.VMEM((1, z.width), jnp.float32),
            pltpu.SemaphoreType.DMA((2 + count,)),
        ],
        compiler_params=pltpu.CompilerParams(vmem_limit_bytes=24 * MIB),
        cost_estimate=COST,
        name="normalise",
    )(meta, tokens, *incoming, gain, bias, *after)


def slot_rows(z, meta, shape, axis):
    index = lax.broadcasted_iota(jnp.int32, shape, axis)
    piece = lax.div(index, jnp.int32(z.rows))
    return (meta[RANK] ^ piece) * z.rows + (index - piece * z.rows)


def members(z, meta, m, rows):
    member = jnp.zeros(rows.shape, jnp.int32)
    for k in range(z.slots):
        member = member + (rows >= meta[z.ends + m * z.slots + k]).astype(jnp.int32)
    return member


def positions(z, meta, m):
    rows = slot_rows(z, meta, (z.rows * z.tensors, 1), 0)
    member = members(z, meta, m, rows)
    start = jnp.zeros(rows.shape, jnp.int32)
    for k in range(1, z.slots):
        start = jnp.where(member == k, meta[z.ends + m * z.slots + k - 1], start)
    return (rows - start).astype(jnp.float32)


def tables(z, meta, m, cosine, sine):
    position = positions(z, meta, m)
    split, half = z.rows * z.tensors // 2, z.size // 2
    lane = lax.broadcasted_iota(jnp.int32, (1, z.size), 1)
    front = lane < half
    index = jnp.where(front, lane, lane - half).astype(jnp.float32)
    frequency = jnp.exp(index * jnp.float32(-2.0 / z.size * 9.210340371976184))
    angle = jnp.where(front, position[:split], position[split:]) * frequency
    c, t = jnp.cos(angle), jnp.sin(angle)
    other_c, other_t = pltpu.roll(c, half, 1), pltpu.roll(t, half, 1)
    cosine[:split, :] = jnp.where(front, c, other_c)
    cosine[split:, :] = jnp.where(front, other_c, c)
    sine[:split, :] = jnp.where(front, -t, other_t)
    sine[split:, :] = jnp.where(front, -other_t, t)


def attend_kernel(z, buckets, later, ready, steps, swaps, book, *rest):
    n, count = z.tensors, len(buckets)
    pieces, rest = rest[:n], rest[n:]
    weight, bias, rest = rest[0], rest[1], rest[2:]
    given, rest = rest[: 2 * ready], rest[2 * ready :]
    earlier, rest = rest[: n * ready], rest[n * ready :]
    before = earlier[0].shape[0] if ready else 0
    outputs, rest = rest[:n], rest[n:]
    made, rest = rest[: 2 * len(later)], rest[2 * len(later) :]
    rows, held, total, cosine, sine, shift, meta, sems, meta_sem = rest
    kept = pltpu.make_async_copy(book, meta, meta_sem)
    full = n * z.rows
    chunk = z.width // steps
    fetches = []
    for s in range(steps):
        at = slice(s * chunk, (s + 1) * chunk)
        now = []
        now.append(pltpu.make_async_copy(weight.at[at], held.at[at], sems.at[s, 0]))
        for i in range(n * count):
            m, j = i // n, i % n
            now.append(
                pltpu.make_async_copy(
                    pieces[j].at[m * z.rows : (m + 1) * z.rows, at],
                    rows.at[i * z.rows : (i + 1) * z.rows, at],
                    sems.at[s, i + 1],
                )
            )
        if s == 0:
            now.append(pltpu.make_async_copy(bias, shift, sems.at[steps, 0]))
        if s == steps - 1 and ready:
            now.append(pltpu.make_async_copy(given[0], cosine.at[0], sems.at[steps, 1]))
            now.append(pltpu.make_async_copy(given[1], sine.at[0], sems.at[steps, 2]))
            for j in range(n):
                now.append(
                    pltpu.make_async_copy(
                        earlier[j], outputs[j].at[0:before], sems.at[steps, 3 + j]
                    )
                )
        for copy in now:
            copy.start()
        if s == 0:
            kept.start()
        fetches.append(now)
    kept.wait()
    if not ready:
        for i, m in enumerate(buckets):
            tables(z, meta, m, cosine.at[i], sine.at[i])
    for i, m in enumerate(later):
        tables(z, meta, m, made[2 * i], made[2 * i + 1])
    for s in range(steps):
        at = slice(s * chunk, (s + 1) * chunk)
        for copy in fetches[s]:
            copy.wait()
        product = jnp.dot(rows[:, at], held[at, :], preferred_element_type=jnp.float32)
        if s == 0:
            total[...] = product + shift[...]
        else:
            total[...] += product
    for i, m in enumerate(buckets):
        row_member = members(z, meta, m, slot_rows(z, meta, (full, 1), 0))
        column_member = members(z, meta, m, slot_rows(z, meta, (1, full), 1))
        allowed = (row_member == column_member) & (column_member < z.slots)
        cos, sin = cosine[i], sine[i]

        def turn(u):
            return (u * cos + pltpu.roll(u, z.size // 2, 1) * sin).astype(jnp.bfloat16)

        def part(kind, h):
            place = (kind * z.heads + h) * z.size
            return total[i * full : (i + 1) * full, place : place + z.size]

        contexts = []
        for h in range(z.heads):
            queries = turn(part(0, h) * jnp.float32(z.size ** (-0.5)))
            key_rows = turn(part(1, h))
            values = part(2, h).astype(jnp.bfloat16)
            scores = lax.dot_general(
                queries, key_rows, (((1,), (1,)), ((), ())), preferred_element_type=jnp.float32
            )
            masked = jnp.where(allowed, scores, jnp.float32(-1e30))
            raised = jnp.exp(masked - jnp.max(masked, axis=-1, keepdims=True))
            share = raised / jnp.sum(raised, axis=-1, keepdims=True)
            contexts.append(
                jnp.dot(share.astype(jnp.bfloat16), values, preferred_element_type=jnp.float32)
            )
        plain = jnp.concatenate(contexts, axis=-1)
        half = z.depth // 2
        turned = plain
        if swaps:
            turned = jnp.concatenate([plain[:, half:], plain[:, :half]], axis=-1)
            turned = jnp.where(meta[PART] == 1, turned, plain)
        for j in range(n):
            value = (turned if j > 1 else plain)[j * z.rows : (j + 1) * z.rows]
            at = before + i * z.rows
            outputs[j][at : at + z.rows, :] = value.astype(jnp.bfloat16)


def attend(z, buckets, later, meta, pieces, weight, bias, given, swaps):
    steps = 2
    count = len(buckets)
    before = given[2].shape[0] if given else 0
    columns = z.kinds * z.depth
    full = z.rows * z.tensors
    table = jax.ShapeDtypeStruct((full, z.size), jnp.float32)
    result = pl.pallas_call(
        functools.partial(attend_kernel, z, buckets, later, bool(given), steps, swaps),
        out_shape=[jax.ShapeDtypeStruct((before + count * z.rows, z.depth), jnp.bfloat16)] * z.tensors
        + [table] * (2 * len(later)),
        in_specs=[ANY] * (z.tensors + 3 + len(given)),
        out_specs=[VMEM] * (z.tensors + 2 * len(later)),
        scratch_shapes=[
            pltpu.VMEM((count * full, z.width), jnp.bfloat16),
            pltpu.VMEM((z.width, columns), jnp.bfloat16),
            pltpu.VMEM((count * full, columns), jnp.float32),
            pltpu.VMEM((count, full, z.size), jnp.float32),
            pltpu.VMEM((count, full, z.size), jnp.float32),
            pltpu.VMEM((1, columns), jnp.float32),
            pltpu.SMEM((z.length,), jnp.int32),
            pltpu.SemaphoreType.DMA((steps + 1, count * z.tensors + 3)),
            pltpu.SemaphoreType.DMA,
        ],
        compiler_params=pltpu.CompilerParams(vmem_limit_bytes=24 * MIB),
        cost_estimate=pl.CostEstimate(
            flops=2 * count * full * z.width * columns,
            bytes_accessed=2 * z.width * (count * full + columns),
            transcendentals=count * z.heads * full * full,
        ),
        name="attend",
    )(meta, *pieces, weight, bias, *given)
    return result[: z.tensors], result[z.tensors :]


def output_kernel(z, depths, counts, steps, meta, *rest):
    contexts, rest = rest[: len(counts) * z.tensors], rest[len(counts) * z.tensors :]
    weights, rest = rest[: len(depths)], rest[len(depths) :]
    tokens, incoming, bias, out = rest[0], rest[1 : 1 + z.moved], rest[1 + z.moved], rest[2 + z.moved]
    held, blocks, joined, ready, shift, sems, block_sems, out_sems, context_sems = rest[3 + z.moved :]
    chunk = z.width // steps
    small = [pltpu.make_async_copy(bias, shift, context_sems.at[0])]
    m = 0
    for g, count in enumerate(counts):
        for j in range(z.tensors):
            small.append(
                pltpu.make_async_copy(
                    contexts[g * z.tensors + j],
                    joined.at[m * z.rows : (m + count) * z.rows, j * z.depth : (j + 1) * z.depth],
                    context_sems.at[len(small)],
                )
            )
        m += count
    for copy in small:
        copy.start()
    fetches = []
    for s in range(steps):
        at = slice(s * chunk, (s + 1) * chunk)
        now = []
        place = 0
        for i, depth in enumerate(depths):
            now.append(
                pltpu.make_async_copy(
                    weights[i].at[:, at], held.at[place : place + depth, at], sems.at[s, i]
                )
            )
            now[-1].start()
            place += depth
        fetches.append(now)
        if s == 0:
            own = [
                pltpu.make_async_copy(
                    tokens.at[meta[z.own + m]], blocks.at[m], block_sems.at[m]
                )
                for m in range(z.count)
            ]
            kept = z.count - z.moved
            other = [
                pltpu.make_async_copy(incoming[k], blocks.at[kept + k], block_sems.at[kept + k])
                for k in range(z.moved)
            ]
            for m in range(kept):
                own[m].start()

            @pl.when(meta[RECEIVES] == 1)
            def _():
                for copy in other:
                    copy.start()

            @pl.when(meta[RECEIVES] != 1)
            def _():
                for copy in own[kept:]:
                    copy.start()

    for copy in small:
        copy.wait()
    index = meta[RANK] * z.rows + lax.broadcasted_iota(jnp.int32, (z.rows, 1), 0)
    leaving = []
    for s in range(steps):
        at = slice(s * chunk, (s + 1) * chunk)
        for copy in fetches[s]:
            copy.wait()
        total = jnp.dot(joined[...], held[:, at], preferred_element_type=jnp.float32)
        if s == 0:
            for copy in own:
                copy.wait()
        for m in range(z.count):
            block = blocks[m, :, at].astype(jnp.float32)
            value = block + total[m * z.rows : (m + 1) * z.rows] + shift[:, at]
            there = index < meta[z.ends + m * z.slots + z.slots - 1]
            ready[m, :, at] = jnp.where(there, value, jnp.float32(0.0)).astype(out.dtype)
            copy = pltpu.make_async_copy(
                ready.at[m, :, at], out.at[meta[z.order + m], :, at], out_sems.at[s, m]
            )
            copy.start()
            leaving.append(copy)
    for copy in leaving:
        copy.wait()


def project(z, meta, contexts, counts, weights, tokens, incoming, bias):
    steps = 5
    depths = [w.shape[0] for w in weights]
    flat = [c for bucket in contexts for c in bucket]
    return pl.pallas_call(
        functools.partial(output_kernel, z, depths, counts, steps),
        out_shape=jax.ShapeDtypeStruct((z.count, z.rows, z.width), tokens.dtype),
        in_specs=[SMEM] + [ANY] * (len(flat) + len(depths) + z.moved + 2),
        out_specs=ANY,
        scratch_shapes=[
            pltpu.VMEM((sum(depths), z.width), jnp.bfloat16),
            pltpu.VMEM((z.count, z.rows, z.width), tokens.dtype),
            pltpu.VMEM((z.count * z.rows, z.tensors * z.depth), jnp.bfloat16),
            pltpu.VMEM((z.count, z.rows, z.width), tokens.dtype),
            pltpu.VMEM((1, z.width), jnp.float32),
            pltpu.SemaphoreType.DMA((steps, len(depths))),
            pltpu.SemaphoreType.DMA((z.count,)),
            pltpu.SemaphoreType.DMA((steps, z.count)),
            pltpu.SemaphoreType.DMA((len(flat) + 1,)),
        ],
        compiler_params=pltpu.CompilerParams(vmem_limit_bytes=14 * MIB + 2 * sum(depths) * z.width),
        cost_estimate=COST,
        name="project",
    )(meta, *flat, *weights, tokens, *incoming, bias)


def on_device(
    tokens, norm_gain, norm_bias, qkv_weight, qkv_bias, out_weight, out_bias, lengths, source_bin
):
    groups = lax.axis_size("dp")
    tensors = lax.axis_size("tensor")
    z = Sizes(tokens, lengths, qkv_weight, groups, tensors)
    flat_out = out_weight.reshape(z.depth, z.width)
    meta, *outgoing, half_out = book(z, source_bin, lengths, tokens, flat_out)

    gain, bias = norm_gain.reshape(1, -1), norm_bias.reshape(1, -1)
    qkv_row = jnp.transpose(qkv_bias, (1, 0, 2)).reshape(1, -1)
    split = lax.axis_size("parts") == 2 and tensors > 2
    kept = z.count - z.moved
    small = tensors <= 4

    def send_back(contexts):
        return [contexts[0]] + [exchange(contexts[j], "tensor", j) for j in range(1, tensors)]

    def relayout(weight):
        flat = jnp.transpose(weight, (0, 2, 1, 3)).reshape(z.width, z.kinds * z.depth)
        return with_layout_constraint(flat, Layout((0, 1)))

    def out_firsts():
        firsts = {0: half_out if split else flat_out}
        for mask in masks_of(tensors)[:-1]:
            for j in list(firsts):
                firsts[j | mask] = exchange(firsts[j], "tensor", mask)
        del firsts[0]
        return firsts

    def across(firsts):
        return {j: exchange(h, "parts", 1) for j, h in firsts.items()} if split else {}

    def work(buckets, pieces, weight, later=(), given=()):
        return attend(z, buckets, later, meta, pieces, weight, qkv_row, given, split)

    def start(buckets, incoming, after=()):
        sources = [incoming[m - kept] for m in buckets if m >= kept]
        return normalise(z, buckets, meta, tokens, sources, gain, bias, after)

    ways = []
    for k in range(1, groups):
        top = 1 << (k.bit_length() - 1)
        up = [(i, i ^ k) for i in range(groups) if not i & top]
        ways += [up, [(d, s) for s, d in up]]

    def choose(branch):
        return lax.switch(meta[CHOSEN], [functools.partial(branch, pairs) for pairs in ways])

    last = z.count - 1
    if small:

        first = list(range(last))

        def early(pairs):
            arrived = [lax.ppermute(block, "dp", pairs) for block in outgoing[:-1]]
            weight = relayout(qkv_weight)
            return arrived, out_firsts(), weight, start(first, arrived, (weight,))

        arrived, firsts, weight, own = choose(early)
        seconds = across(firsts)

        def late(pairs):
            arriving = lax.ppermute(outgoing[-1], "dp", pairs)
            crossed = hop(own)
            beside = exchange(own, "tensor", 1)
            return arriving, crossed, beside, start([last], arrived + [arriving])

        arriving, crossed, beside, normed = choose(late)
        held = gather_xor(own, crossed, None, beside)
        incoming = arrived + [arriving]
        normed, seconds = lax.optimization_barrier((normed, seconds))
        counts = [z.count]
        context, made = work(first, held, weight, [last])
        pieces = gather_xor(normed, None, context[0])
        context, _ = work([last], pieces, weight, (), [*made, *context])
        contexts = [send_back(context)]
    else:
        incoming = choose(lambda pairs: [lax.ppermute(b, "dp", pairs) for b in outgoing])
        weight = relayout(qkv_weight)
        firsts = out_firsts()
        seconds = across(firsts)
        counts = [1] * z.count
        contexts = [
            send_back(work([m], gather_xor(start([m], incoming)), weight)[0])
            for m in range(z.count)
        ]

    rows_of = {0: [flat_out]}
    if tensors > 1:
        rows_of[1] = [exchange(flat_out, "tensor", 1)]
    for j in firsts:
        held = [firsts[j]]
        rows_of[j | 1] = [exchange(firsts[j], "tensor", 1)]
        if split:
            second = seconds[j]
            held.append(second)
            second, _ = lax.optimization_barrier((second, contexts[-1][0]))
            rows_of[j | 1].append(exchange(second, "tensor", 1))
        rows_of[j] = held
    weights = [h for j in range(tensors) for h in rows_of[j]]
    return project(z, meta, contexts, counts, weights, tokens, incoming, out_bias.reshape(1, -1))


def solution(mesh):
    return jax.shard_map(
        on_device,
        mesh=mesh,
        in_specs=(
            P(("parts", "dp"), "tensor", None),
            P(),
            P(),
            P(None, "tensor", None, None),
            P("tensor", None, None),
            P("tensor", None, None),
            P(),
            P("parts", None),
            P("parts"),
        ),
        out_specs=P(("parts", "dp"), "tensor", None),
        check_vma=False,
    )
```

```python
import functools

import jax
import jax.numpy as jnp
from jax import lax
from jax.experimental import pallas as pl
from jax.experimental.layout import Layout, with_layout_constraint
from jax.experimental.pallas import tpu as pltpu
from jax.sharding import PartitionSpec as P

MIB = 1 << 20
COST = pl.CostEstimate(flops=0, bytes_accessed=0, transcendentals=0)
CHOSEN, RECEIVES, GROUP, RANK, PART, FIRST = 0, 1, 2, 3, 4, 8
ANY = pl.BlockSpec(memory_space=pl.ANY)
SMEM = pl.BlockSpec(memory_space=pltpu.SMEM)
VMEM = pl.BlockSpec(memory_space=pltpu.VMEM)


def exchange(value, axis, mask):
    size = lax.axis_size(axis)
    return lax.ppermute(value, axis, [(i, i ^ mask) for i in range(size)])


def masks_of(size):
    mask = size // 2
    result = []
    while mask:
        result.append(mask)
        mask //= 2
    return result


def hop(own):
    return exchange(own, "tensor", lax.axis_size("tensor") // 2)


def gather_xor(own, crossed=None, after=None):
    pieces = {0: own}
    for mask in masks_of(lax.axis_size("tensor")):
        for j in list(pieces):
            piece = pieces[j]
            if crossed is not None and len(pieces) == 1:
                pieces[j | mask] = crossed
                continue
            if j and after is not None:
                piece, _ = lax.optimization_barrier((piece, after))
            pieces[j | mask] = exchange(piece, "tensor", mask)
    return [pieces[j] for j in range(len(pieces))]


class Sizes:
    def __init__(self, tokens, lengths, qkv_weight, groups, tensors):
        self.bins, self.rows, self.width = tokens.shape
        self.slots = lengths.shape[-1]
        self.buckets = lengths.shape[0]
        self.groups = groups
        self.tensors = tensors
        self.count = self.buckets // groups
        self.moved = self.bins - self.count
        self.heads, self.kinds, self.size = qkv_weight.shape[1:]
        self.depth = self.heads * self.size
        self.order = FIRST
        self.own = self.order + self.count
        self.sent = self.own + self.count
        self.ends = self.sent + self.moved + 1
        self.length = self.ends + self.count * self.slots


def book_kernel(z, source, lengths, tokens, out_weight, meta, *rest):
    outgoing, first, sems = rest[:-2], rest[-2], rest[-1]
    ids = [lax.axis_index(axis) for axis in ("dp", "tensor", "parts")]
    group = ids[0]
    deep = first.shape[0]
    copies = [
        pltpu.make_async_copy(
            out_weight.at[pl.ds(pl.multiple_of(ids[2] * deep, deep), deep)],
            first,
            sems.at[z.moved],
        )
    ]
    copies[0].start()
    for i in range(z.length):
        meta[i] = jnp.int32(0)
    sent = jnp.int32(0)
    partner = jnp.int32(0)
    for b in range(z.buckets):
        owner = b // z.count
        place = source[b] - group * z.bins
        here = (place >= 0) & (place < z.bins) & (owner != group)
        meta[z.sent + jnp.where(here, jnp.minimum(sent, z.moved), z.moved)] = jnp.where(
            here, place, 0
        )
        sent = sent + here.astype(jnp.int32)
        partner = jnp.where(here, owner, partner)
    for m in range(z.moved):
        copies.append(
            pltpu.make_async_copy(tokens.at[meta[z.sent + m]], outgoing[m], sems.at[m])
        )
        copies[-1].start()
    leaving = []
    for m in range(z.count):
        place = source[group * z.count + m] - group * z.bins
        leaving.append(((place < 0) | (place >= z.bins)).astype(jnp.int32))
    left_total = functools.reduce(lambda a, b: a + b, leaving)
    kept_before = jnp.int32(0)
    left_before = z.count - left_total
    for m in range(z.count):
        bucket = group * z.count + m
        leaves = leaving[m] == 1
        place = jnp.where(leaves, left_before, kept_before)
        meta[z.order + place] = jnp.int32(m)
        meta[z.own + place] = jnp.where(leaves, 0, source[bucket] - group * z.bins)
        partner = jnp.where(leaves, lax.div(source[bucket], jnp.int32(z.bins)), partner)
        end = jnp.int32(0)
        for k in range(z.slots):
            end = end + lengths[k, bucket]
            meta[z.ends + place * z.slots + k] = end
        kept_before = kept_before + (1 - leaving[m])
        left_before = left_before + leaving[m]
    receives = left_total > 0
    apart = group ^ partner
    top = jnp.int32(1)
    for k in range(1, z.groups):
        top = jnp.where(apart == k, 1 << (k.bit_length() - 1), top)
    sender = jnp.where(receives, partner, group)
    down = ((sender & top) != 0).astype(jnp.int32)
    meta[CHOSEN] = 2 * jnp.maximum(apart - 1, 0) + down
    meta[RECEIVES] = receives.astype(jnp.int32)
    for i in range(3):
        meta[GROUP + i] = ids[i]
    for copy in copies:
        copy.wait()


def book(z, source_bin, lengths, tokens, flat_out):
    block = jax.ShapeDtypeStruct((z.rows, z.width), tokens.dtype)
    first = jax.ShapeDtypeStruct((z.depth // 2, z.width), flat_out.dtype)
    return pl.pallas_call(
        functools.partial(book_kernel, z),
        out_shape=[jax.ShapeDtypeStruct((z.length,), jnp.int32)] + [block] * z.moved + [first],
        in_specs=[SMEM, SMEM, ANY, ANY],
        out_specs=[SMEM] + [VMEM] * (z.moved + 1),
        scratch_shapes=[pltpu.SemaphoreType.DMA((z.moved + 1,))],
        compiler_params=pltpu.CompilerParams(vmem_limit_bytes=60 * MIB),
        cost_estimate=COST,
        name="book",
    )(source_bin, lengths.T, tokens, flat_out)


def norm_kernel(z, buckets, after, meta, tokens, *rest):
    kept = z.count - z.moved
    arrived = sum(m >= kept for m in buckets)
    incoming, rest = rest[:arrived], rest[arrived:]
    affine = rest[:2]
    normed, blocks, gain, bias, sems = rest[2 + after :]
    copies = [
        pltpu.make_async_copy(affine[0], gain, sems.at[0]),
        pltpu.make_async_copy(affine[1], bias, sems.at[1]),
    ]
    for copy in copies:
        copy.start()
    own, other = [], {}
    for i, m in enumerate(buckets):
        own.append(
            pltpu.make_async_copy(tokens.at[meta[z.own + m]], blocks.at[i], sems.at[2 + i])
        )
        if m < kept:
            own[-1].start()
        else:
            source = incoming[len(other)]
            other[i] = pltpu.make_async_copy(source, blocks.at[i], sems.at[2 + i])
    if other:

        @pl.when(meta[RECEIVES] == 1)
        def _():
            for copy in other.values():
                copy.start()

        @pl.when(meta[RECEIVES] != 1)
        def _():
            for i in other:
                own[i].start()

    for copy in copies:
        copy.wait()
    step = 16
    for i in range(len(buckets)):
        own[i].wait()
        for r in range(0, z.rows, step):
            widened = blocks[i, r : r + step, :].astype(jnp.float32)
            average = jnp.mean(widened, axis=-1, keepdims=True)
            centred = widened - average
            spread = jnp.mean(centred * centred, axis=-1, keepdims=True)
            scaled = centred * lax.rsqrt(spread + 1e-05) * gain[...] + bias[...]
            at = i * z.rows + r
            normed[at : at + step, :] = scaled.astype(normed.dtype)


def normalise(z, buckets, meta, tokens, incoming, gain, bias, after=()):
    count = len(buckets)
    return pl.pallas_call(
        functools.partial(norm_kernel, z, buckets, len(after)),
        out_shape=jax.ShapeDtypeStruct((count * z.rows, z.width), tokens.dtype),
        in_specs=[SMEM, ANY] + [ANY] * (len(incoming) + 2 + len(after)),
        out_specs=VMEM,
        scratch_shapes=[
            pltpu.VMEM((count, z.rows, z.width), tokens.dtype),
            pltpu.VMEM((1, z.width), jnp.float32),
            pltpu.VMEM((1, z.width), jnp.float32),
            pltpu.SemaphoreType.DMA((2 + count,)),
        ],
        compiler_params=pltpu.CompilerParams(vmem_limit_bytes=24 * MIB),
        cost_estimate=COST,
        name="normalise",
    )(meta, tokens, *incoming, gain, bias, *after)


def slot_rows(z, meta, shape, axis):
    index = lax.broadcasted_iota(jnp.int32, shape, axis)
    piece = lax.div(index, jnp.int32(z.rows))
    return (meta[RANK] ^ piece) * z.rows + (index - piece * z.rows)


def members(z, meta, m, rows):
    member = jnp.zeros(rows.shape, jnp.int32)
    for k in range(z.slots):
        member = member + (rows >= meta[z.ends + m * z.slots + k]).astype(jnp.int32)
    return member


def positions(z, meta, m):
    rows = slot_rows(z, meta, (z.rows * z.tensors, 1), 0)
    member = members(z, meta, m, rows)
    start = jnp.zeros(rows.shape, jnp.int32)
    for k in range(1, z.slots):
        start = jnp.where(member == k, meta[z.ends + m * z.slots + k - 1], start)
    return (rows - start).astype(jnp.float32)


def tables(z, meta, m, cosine, sine):
    position = positions(z, meta, m)
    split, half = z.rows * z.tensors // 2, z.size // 2
    lane = lax.broadcasted_iota(jnp.int32, (1, z.size), 1)
    front = lane < half
    index = jnp.where(front, lane, lane - half).astype(jnp.float32)
    frequency = jnp.exp(index * jnp.float32(-2.0 / z.size * 9.210340371976184))
    angle = jnp.where(front, position[:split], position[split:]) * frequency
    c, t = jnp.cos(angle), jnp.sin(angle)
    other_c, other_t = pltpu.roll(c, half, 1), pltpu.roll(t, half, 1)
    cosine[:split, :] = jnp.where(front, c, other_c)
    cosine[split:, :] = jnp.where(front, other_c, c)
    sine[:split, :] = jnp.where(front, -t, other_t)
    sine[split:, :] = jnp.where(front, -other_t, t)


def attend_kernel(z, buckets, later, ready, steps, swaps, book, *rest):
    n, count = z.tensors, len(buckets)
    pieces, rest = rest[:n], rest[n:]
    weight, bias, rest = rest[0], rest[1], rest[2:]
    given, rest = rest[: 2 * ready], rest[2 * ready :]
    earlier, rest = rest[: n * ready], rest[n * ready :]
    before = earlier[0].shape[0] if ready else 0
    outputs, rest = rest[:n], rest[n:]
    made, rest = rest[: 2 * len(later)], rest[2 * len(later) :]
    rows, held, total, cosine, sine, shift, meta, sems, meta_sem = rest
    kept = pltpu.make_async_copy(book, meta, meta_sem)
    full = n * z.rows
    chunk = z.width // steps
    fetches = []
    for s in range(steps):
        at = slice(s * chunk, (s + 1) * chunk)
        now = []
        now.append(pltpu.make_async_copy(weight.at[at], held.at[at], sems.at[s, 0]))
        for i in range(n * count):
            m, j = i // n, i % n
            now.append(
                pltpu.make_async_copy(
                    pieces[j].at[m * z.rows : (m + 1) * z.rows, at],
                    rows.at[i * z.rows : (i + 1) * z.rows, at],
                    sems.at[s, i + 1],
                )
            )
        if s == 0:
            now.append(pltpu.make_async_copy(bias, shift, sems.at[steps, 0]))
        if s == steps - 1 and ready:
            now.append(pltpu.make_async_copy(given[0], cosine.at[0], sems.at[steps, 1]))
            now.append(pltpu.make_async_copy(given[1], sine.at[0], sems.at[steps, 2]))
            for j in range(n):
                now.append(
                    pltpu.make_async_copy(
                        earlier[j], outputs[j].at[0:before], sems.at[steps, 3 + j]
                    )
                )
        for copy in now:
            copy.start()
        if s == 0:
            kept.start()
        fetches.append(now)
    kept.wait()
    if not ready:
        for i, m in enumerate(buckets):
            tables(z, meta, m, cosine.at[i], sine.at[i])
    for i, m in enumerate(later):
        tables(z, meta, m, made[2 * i], made[2 * i + 1])
    for s in range(steps):
        at = slice(s * chunk, (s + 1) * chunk)
        for copy in fetches[s]:
            copy.wait()
        product = jnp.dot(rows[:, at], held[at, :], preferred_element_type=jnp.float32)
        if s == 0:
            total[...] = product + shift[...]
        else:
            total[...] += product
    for i, m in enumerate(buckets):
        row_member = members(z, meta, m, slot_rows(z, meta, (full, 1), 0))
        column_member = members(z, meta, m, slot_rows(z, meta, (1, full), 1))
        allowed = (row_member == column_member) & (column_member < z.slots)
        cos, sin = cosine[i], sine[i]

        def turn(u):
            return (u * cos + pltpu.roll(u, z.size // 2, 1) * sin).astype(jnp.bfloat16)

        def part(kind, h):
            place = (kind * z.heads + h) * z.size
            return total[i * full : (i + 1) * full, place : place + z.size]

        contexts = []
        for h in range(z.heads):
            queries = turn(part(0, h) * jnp.float32(z.size ** (-0.5)))
            key_rows = turn(part(1, h))
            values = part(2, h).astype(jnp.bfloat16)
            scores = lax.dot_general(
                queries, key_rows, (((1,), (1,)), ((), ())), preferred_element_type=jnp.float32
            )
            masked = jnp.where(allowed, scores, jnp.float32(-1e30))
            raised = jnp.exp(masked - jnp.max(masked, axis=-1, keepdims=True))
            share = raised / jnp.sum(raised, axis=-1, keepdims=True)
            contexts.append(
                jnp.dot(share.astype(jnp.bfloat16), values, preferred_element_type=jnp.float32)
            )
        plain = jnp.concatenate(contexts, axis=-1)
        half = z.depth // 2
        turned = plain
        if swaps:
            turned = jnp.concatenate([plain[:, half:], plain[:, :half]], axis=-1)
            turned = jnp.where(meta[PART] == 1, turned, plain)
        for j in range(n):
            value = (turned if j > 1 else plain)[j * z.rows : (j + 1) * z.rows]
            at = before + i * z.rows
            outputs[j][at : at + z.rows, :] = value.astype(jnp.bfloat16)


def attend(z, buckets, later, meta, pieces, weight, bias, given, swaps):
    steps = 2
    count = len(buckets)
    before = given[2].shape[0] if given else 0
    columns = z.kinds * z.depth
    full = z.rows * z.tensors
    table = jax.ShapeDtypeStruct((full, z.size), jnp.float32)
    result = pl.pallas_call(
        functools.partial(attend_kernel, z, buckets, later, bool(given), steps, swaps),
        out_shape=[jax.ShapeDtypeStruct((before + count * z.rows, z.depth), jnp.bfloat16)] * z.tensors
        + [table] * (2 * len(later)),
        in_specs=[ANY] * (z.tensors + 3 + len(given)),
        out_specs=[VMEM] * (z.tensors + 2 * len(later)),
        scratch_shapes=[
            pltpu.VMEM((count * full, z.width), jnp.bfloat16),
            pltpu.VMEM((z.width, columns), jnp.bfloat16),
            pltpu.VMEM((count * full, columns), jnp.float32),
            pltpu.VMEM((count, full, z.size), jnp.float32),
            pltpu.VMEM((count, full, z.size), jnp.float32),
            pltpu.VMEM((1, columns), jnp.float32),
            pltpu.SMEM((z.length,), jnp.int32),
            pltpu.SemaphoreType.DMA((steps + 1, count * z.tensors + 3)),
            pltpu.SemaphoreType.DMA,
        ],
        compiler_params=pltpu.CompilerParams(vmem_limit_bytes=24 * MIB),
        cost_estimate=pl.CostEstimate(
            flops=2 * count * full * z.width * columns,
            bytes_accessed=2 * z.width * (count * full + columns),
            transcendentals=count * z.heads * full * full,
        ),
        name="attend",
    )(meta, *pieces, weight, bias, *given)
    return result[: z.tensors], result[z.tensors :]


def output_kernel(z, depths, counts, steps, meta, *rest):
    contexts, rest = rest[: len(counts) * z.tensors], rest[len(counts) * z.tensors :]
    weights, rest = rest[: len(depths)], rest[len(depths) :]
    tokens, incoming, bias, out = rest[0], rest[1 : 1 + z.moved], rest[1 + z.moved], rest[2 + z.moved]
    held, blocks, joined, ready, shift, sems, block_sems, out_sems, context_sems = rest[3 + z.moved :]
    chunk = z.width // steps
    small = [pltpu.make_async_copy(bias, shift, context_sems.at[0])]
    m = 0
    for g, count in enumerate(counts):
        for j in range(z.tensors):
            small.append(
                pltpu.make_async_copy(
                    contexts[g * z.tensors + j],
                    joined.at[m * z.rows : (m + count) * z.rows, j * z.depth : (j + 1) * z.depth],
                    context_sems.at[len(small)],
                )
            )
        m += count
    for copy in small:
        copy.start()
    fetches = []
    for s in range(steps):
        at = slice(s * chunk, (s + 1) * chunk)
        now = []
        place = 0
        for i, depth in enumerate(depths):
            now.append(
                pltpu.make_async_copy(
                    weights[i].at[:, at], held.at[place : place + depth, at], sems.at[s, i]
                )
            )
            now[-1].start()
            place += depth
        fetches.append(now)
        if s == 0:
            own = [
                pltpu.make_async_copy(
                    tokens.at[meta[z.own + m]], blocks.at[m], block_sems.at[m]
                )
                for m in range(z.count)
            ]
            kept = z.count - z.moved
            other = [
                pltpu.make_async_copy(incoming[k], blocks.at[kept + k], block_sems.at[kept + k])
                for k in range(z.moved)
            ]
            for m in range(kept):
                own[m].start()

            @pl.when(meta[RECEIVES] == 1)
            def _():
                for copy in other:
                    copy.start()

            @pl.when(meta[RECEIVES] != 1)
            def _():
                for copy in own[kept:]:
                    copy.start()

    for copy in small:
        copy.wait()
    index = meta[RANK] * z.rows + lax.broadcasted_iota(jnp.int32, (z.rows, 1), 0)
    leaving = []
    for s in range(steps):
        at = slice(s * chunk, (s + 1) * chunk)
        for copy in fetches[s]:
            copy.wait()
        total = jnp.dot(joined[...], held[:, at], preferred_element_type=jnp.float32)
        if s == 0:
            for copy in own:
                copy.wait()
        for m in range(z.count):
            block = blocks[m, :, at].astype(jnp.float32)
            value = block + total[m * z.rows : (m + 1) * z.rows] + shift[:, at]
            there = index < meta[z.ends + m * z.slots + z.slots - 1]
            ready[m, :, at] = jnp.where(there, value, jnp.float32(0.0)).astype(out.dtype)
            copy = pltpu.make_async_copy(
                ready.at[m, :, at], out.at[meta[z.order + m], :, at], out_sems.at[s, m]
            )
            copy.start()
            leaving.append(copy)
    for copy in leaving:
        copy.wait()


def project(z, meta, contexts, counts, weights, tokens, incoming, bias):
    steps = 5
    depths = [w.shape[0] for w in weights]
    flat = [c for bucket in contexts for c in bucket]
    return pl.pallas_call(
        functools.partial(output_kernel, z, depths, counts, steps),
        out_shape=jax.ShapeDtypeStruct((z.count, z.rows, z.width), tokens.dtype),
        in_specs=[SMEM] + [ANY] * (len(flat) + len(depths) + z.moved + 2),
        out_specs=ANY,
        scratch_shapes=[
            pltpu.VMEM((sum(depths), z.width), jnp.bfloat16),
            pltpu.VMEM((z.count, z.rows, z.width), tokens.dtype),
            pltpu.VMEM((z.count * z.rows, z.tensors * z.depth), jnp.bfloat16),
            pltpu.VMEM((z.count, z.rows, z.width), tokens.dtype),
            pltpu.VMEM((1, z.width), jnp.float32),
            pltpu.SemaphoreType.DMA((steps, len(depths))),
            pltpu.SemaphoreType.DMA((z.count,)),
            pltpu.SemaphoreType.DMA((steps, z.count)),
            pltpu.SemaphoreType.DMA((len(flat) + 1,)),
        ],
        compiler_params=pltpu.CompilerParams(vmem_limit_bytes=14 * MIB + 2 * sum(depths) * z.width),
        cost_estimate=COST,
        name="project",
    )(meta, *flat, *weights, tokens, *incoming, bias)


def on_device(
    tokens, norm_gain, norm_bias, qkv_weight, qkv_bias, out_weight, out_bias, lengths, source_bin
):
    groups = lax.axis_size("dp")
    tensors = lax.axis_size("tensor")
    z = Sizes(tokens, lengths, qkv_weight, groups, tensors)
    flat_out = out_weight.reshape(z.depth, z.width)
    meta, *outgoing, half_out = book(z, source_bin, lengths, tokens, flat_out)

    gain, bias = norm_gain.reshape(1, -1), norm_bias.reshape(1, -1)
    qkv_row = jnp.transpose(qkv_bias, (1, 0, 2)).reshape(1, -1)
    split = lax.axis_size("parts") == 2 and tensors > 2
    kept = z.count - z.moved
    small = tensors <= 4

    def send_back(contexts):
        return [contexts[0]] + [exchange(contexts[j], "tensor", j) for j in range(1, tensors)]

    def relayout(weight):
        flat = jnp.transpose(weight, (0, 2, 1, 3)).reshape(z.width, z.kinds * z.depth)
        return with_layout_constraint(flat, Layout((0, 1)))

    def out_firsts():
        firsts = {0: half_out if split else flat_out}
        for mask in masks_of(tensors)[:-1]:
            for j in list(firsts):
                firsts[j | mask] = exchange(firsts[j], "tensor", mask)
        del firsts[0]
        return firsts

    def across(firsts):
        return {j: exchange(h, "parts", 1) for j, h in firsts.items()} if split else {}

    def work(buckets, pieces, weight, later=(), given=()):
        return attend(z, buckets, later, meta, pieces, weight, qkv_row, given, split)

    def start(buckets, incoming, after=()):
        sources = [incoming[m - kept] for m in buckets if m >= kept]
        return normalise(z, buckets, meta, tokens, sources, gain, bias, after)

    ways = []
    for k in range(1, groups):
        top = 1 << (k.bit_length() - 1)
        up = [(i, i ^ k) for i in range(groups) if not i & top]
        ways += [up, [(d, s) for s, d in up]]

    def choose(branch):
        return lax.switch(meta[CHOSEN], [functools.partial(branch, pairs) for pairs in ways])

    last = z.count - 1
    if small:

        first = list(range(last))

        def early(pairs):
            arrived = [lax.ppermute(block, "dp", pairs) for block in outgoing[:-1]]
            weight = relayout(qkv_weight)
            return arrived, out_firsts(), weight, start(first, arrived, (weight,))

        arrived, firsts, weight, own = choose(early)
        seconds = across(firsts)

        def late(pairs):
            arriving = lax.ppermute(outgoing[-1], "dp", pairs)
            return arriving, hop(own)

        arriving, crossed = choose(late)
        held = gather_xor(own, crossed)
        incoming = arrived + [arriving]
        normed = start([last], incoming, list(seconds.values()))
        counts = [z.count]
        context, made = work(first, held, weight, [last])
        pieces = gather_xor(normed, None, context[0])
        context, _ = work([last], pieces, weight, (), [*made, *context])
        contexts = [send_back(context)]
    else:
        incoming = choose(lambda pairs: [lax.ppermute(b, "dp", pairs) for b in outgoing])
        weight = relayout(qkv_weight)
        firsts = out_firsts()
        seconds = across(firsts)
        counts = [1] * z.count
        contexts = [
            send_back(work([m], gather_xor(start([m], incoming)), weight)[0])
            for m in range(z.count)
        ]

    rows_of = {0: [flat_out]}
    if tensors > 1:
        rows_of[1] = [exchange(flat_out, "tensor", 1)]
    for j in firsts:
        held = [firsts[j]]
        rows_of[j | 1] = [exchange(firsts[j], "tensor", 1)]
        if split:
            second = seconds[j]
            held.append(second)
            second, _ = lax.optimization_barrier((second, contexts[-1][0]))
            rows_of[j | 1].append(exchange(second, "tensor", 1))
        rows_of[j] = held
    weights = [h for j in range(tensors) for h in rows_of[j]]
    return project(z, meta, contexts, counts, weights, tokens, incoming, out_bias.reshape(1, -1))


def solution(mesh):
    return jax.shard_map(
        on_device,
        mesh=mesh,
        in_specs=(
            P(("parts", "dp"), "tensor", None),
            P(),
            P(),
            P(None, "tensor", None, None),
            P("tensor", None, None),
            P("tensor", None, None),
            P(),
            P("parts", None),
            P("parts"),
        ),
        out_specs=P(("parts", "dp"), "tensor", None),
        check_vma=False,
    )
```
